256 devices in a mesh: theta: 64 (over y_lo, x, z), row: 4 (over y_hi, core).
Axes of the slice: x: 4, y: 4 (y_hi: 2, y_lo: 2; y = y_hi * 2 + y_lo), z: 8, core: 2. Of those that a mesh axis runs over, the one named last changes fastest.
Arguments:
- velocity: float32 [3, 512, 1536, 128], P(None, 'theta', 'row'), may hold values from -5 to 5
Outputs:
- radial_part: bfloat16 [3, 512, 1536, 128], P(None, 'theta', 'row')
- azimuthal_part: bfloat16 [3, 512, 1536, 128], P(None, 'theta', 'row')
The draws below stay inside these ranges and needn't reach their ends.
All inputs are finite; a program needn't handle non-finite values.
Results may differ from the reference program's by a relative error of at most 0.001.
Values sent between devices are 32-bit elements; how exact they have to be, the bound alone decides.
A program may use at most 192 MiB of HBM per device.

```python
import math
import jax
import jax.numpy as jnp
from jax import lax

Z = 128
NR = 1536
NT = 512
N_THETA = 64


def block_scale(stream_key, shape, pieces, least, high):
    gain, own = 1.0, jax.random.fold_in(stream_key, 6)
    for dim, shards_of in pieces:
        draws = jnp.exp(jax.random.uniform(jax.random.fold_in(own, dim), (shards_of,), jnp.float32, least / len(pieces), high / len(pieces)))
        gain = gain * jnp.repeat(draws, shape[dim] // shards_of).reshape([-1 if axis == dim else 1 for axis in range(len(shape))])
    return gain


def bell_draw(own_key, extent, scale, bound, split=(), dtype=jnp.bfloat16):
    gain = block_scale(own_key, extent, split, -0.22, 0.18) if split else 1.0
    drawn = jax.random.normal(own_key, extent, jnp.float32) * scale * gain
    return jnp.minimum(jnp.maximum(drawn, -bound), bound).astype(dtype)


def setup_inputs(seed: int = 0) -> dict:
    seeds = jax.random.split(jax.random.key(seed), 2)
    velocity = bell_draw(seeds[0], (3, NT, NR, Z), 1.0, 5.0, ((1, 64), (2, 4)), jnp.float32)
    return dict(velocity=velocity)


def tendencies(velocity, radial_ext, azimuth_ext, shell_pos, grid_r, grid_t):
    spacing = 1.0 / grid_r
    angle_step = 2.0 * math.pi / grid_t
    axial_step = 4.0 / grid_r
    viscosity = 0.5 / grid_r
    time_step = 0.2 / grid_r
    angle_time = 2.0 / grid_r
    radius = (shell_pos + 0.5) * spacing
    radial_slope = (8.0 * (radial_ext[:, :, 3:-1] - radial_ext[:, :, 1:-3]) - (radial_ext[:, :, 4:] - radial_ext[:, :, :-4])) / (12.0 * spacing)
    radial_lap = ((shell_pos + 1.0) * (radial_ext[:, :, 3:-1] - velocity) - shell_pos * (velocity - radial_ext[:, :, 1:-3])) / ((shell_pos + 0.5) * spacing * spacing)
    angle_slope = (8.0 * (azimuth_ext[:, 3:-1] - azimuth_ext[:, 1:-3]) - (azimuth_ext[:, 4:] - azimuth_ext[:, :-4])) / (12.0 * angle_step)
    angle_lap = (azimuth_ext[:, 3:-1] - 2.0 * velocity + azimuth_ext[:, 1:-3]) / (angle_step * angle_step)
    ahead_one = jnp.roll(velocity, -1, axis=3)
    behind_one = jnp.roll(velocity, 1, axis=3)
    ahead_two = jnp.roll(velocity, -2, axis=3)
    behind_two = jnp.roll(velocity, 2, axis=3)
    axial_slope = (8.0 * (ahead_one - behind_one) - (ahead_two - behind_two)) / (12.0 * axial_step)
    axial_lap = (ahead_one - 2.0 * velocity + behind_one) / (axial_step * axial_step)
    u_rad = velocity[0]
    u_ang = velocity[1]
    u_ax = velocity[2]
    radial_part = time_step * (-(u_rad * radial_slope + u_ax * axial_slope) + viscosity * (radial_lap + axial_lap))
    zeros = jnp.zeros_like(u_rad)
    curvature = jnp.stack([radius * u_ang * u_ang, -radius * u_rad * u_ang, zeros])
    metric = jnp.stack([-u_rad - 2.0 * angle_slope[1], -u_ang + 2.0 * angle_slope[0], zeros])
    azimuthal_part = angle_time * (-radius * u_ang * angle_slope + curvature + viscosity * (angle_lap + metric))
    return radial_part.astype(jnp.bfloat16), azimuthal_part.astype(jnp.bfloat16)


def reference(velocity):
    grid_t = velocity.shape[1]
    grid_r = velocity.shape[2]
    planes = velocity.shape[3]
    width = grid_t // N_THETA
    parity = jnp.array([-1.0, -1.0, 1.0], jnp.float32).reshape(3, 1, 1, 1)
    shell_pos = jnp.arange(grid_r).astype(jnp.float32).reshape(grid_r, 1)
    inner_rows = velocity[:, :, :2]

    def block(start):
        columns = ((start - 2 + jnp.arange(width + 4)) % grid_t).astype(jnp.int32)
        columns_block = jnp.take(velocity, columns, axis=1)
        facing = jnp.take(inner_rows, ((columns + grid_t // 2) % grid_t).astype(jnp.int32), axis=1)
        extended = jnp.concatenate([parity * facing[:, :, ::-1], columns_block, -columns_block[:, :, grid_r - 2:][:, :, ::-1]], axis=2)
        return tendencies(extended[:, 2:-2, 2:-2], extended[:, 2:-2, :], extended[:, :, 2:-2], shell_pos, grid_r, grid_t)

    radial_all, azimuth_all = lax.map(block, (jnp.arange(N_THETA) * width).astype(jnp.int32))
    radial_part = jnp.moveaxis(radial_all, 0, 1).reshape(3, grid_t, grid_r, planes)
    azimuthal_part = jnp.moveaxis(azimuth_all, 0, 1).reshape(3, grid_t, grid_r, planes)
    return radial_part, azimuthal_part
```

```python
import functools
import math

import jax
import jax.numpy as jnp
from jax import lax
from jax.experimental import pallas as pl
from jax.experimental.pallas import tpu as pltpu
from jax.sharding import PartitionSpec as P

MESH = pl.DeviceIdType.MESH
PAD = 8
BLOCK = 32
PIECES = 4


def radial_block(ext, weights, out, m, row, grid_r):
    slope_r = 0.2 / 12.0
    slope_z = 0.2 / 48.0
    lap_r = 0.1
    lap_z = 0.1 / 16.0
    mid = pl.ds(row + PAD, BLOCK)
    inverse = weights[0, pl.ds(row, BLOCK), :]
    u_rad = ext[0, m + 2, mid, :]
    u_ax = ext[2, m + 2, mid, :]
    radial_two = u_rad * (-slope_r)
    radial_one = radial_two * 8.0 + lap_r * inverse
    axial_two = u_ax * (-slope_z)
    axial_one = axial_two * 8.0
    for c in range(3):
        f = ext[c, m + 2, mid, :]
        out_one = ext[c, m + 2, pl.ds(row + PAD + 1, BLOCK), :]
        in_one = ext[c, m + 2, pl.ds(row + PAD - 1, BLOCK), :]
        out_two = ext[c, m + 2, pl.ds(row + PAD + 2, BLOCK), :]
        in_two = ext[c, m + 2, pl.ds(row + PAD - 2, BLOCK), :]
        planes = f.shape[1]
        ahead_one = pltpu.roll(f, planes - 1, 1)
        behind_one = pltpu.roll(f, 1, 1)
        ahead_two = pltpu.roll(f, planes - 2, 1)
        behind_two = pltpu.roll(f, 2, 1)
        total = (out_one - in_one) * radial_one - (out_two - in_two) * radial_two
        total += (ahead_one - behind_one) * axial_one - (ahead_two - behind_two) * axial_two
        total += (out_one + in_one) * lap_r + (ahead_one + behind_one) * lap_z
        total -= f * (2.0 * (lap_r + lap_z))
        out[c, m, pl.ds(row, BLOCK), :] = total.astype(out.dtype)


def azimuth_block(ext, weights, out, m, row, grid_r, grid_t):
    step = 2.0 * math.pi / grid_t
    angle_time = 2.0 / grid_r
    small = angle_time * 0.5 / grid_r
    lap = small / (step * step)
    slope = 8.0 / (12.0 * step)
    mid = pl.ds(row + PAD, BLOCK)
    radius = weights[1, pl.ds(row, BLOCK), :] * angle_time
    u_rad = ext[0, m + 2, mid, :]
    u_ang = ext[1, m + 2, mid, :]
    carried = radius * u_ang
    slopes, totals = [], []
    for c in range(3):
        f = u_rad if c == 0 else u_ang if c == 1 else ext[c, m + 2, mid, :]
        up = ext[c, m + 3, mid, :]
        down = ext[c, m + 1, mid, :]
        wide = ext[c, m + 4, mid, :] - ext[c, m, mid, :]
        slopes.append(((up - down) - wide * 0.125) * slope)
        totals.append((up + down) * lap - f * (2.0 * lap if c == 2 else 2.0 * lap + small))
    totals[0] += carried * (u_ang - slopes[0]) - slopes[1] * (2.0 * small)
    totals[1] += slopes[0] * (2.0 * small) - carried * (u_rad + slopes[1])
    totals[2] -= carried * slopes[2]
    for c in range(3):
        out[c, m, pl.ds(row, BLOCK), :] = totals[c].astype(out.dtype)


def tendencies(loop_size, shells, v, radial, azimuth, ext, weights, own_sem, send_sem, recv_sem, ghost_send, ghost_recv):
    width, rows = v.shape[1], v.shape[2]
    grid_r, grid_t = rows * shells, width * loop_size
    top = rows + PAD
    t = lax.axis_index("theta")
    shell = lax.axis_index("row")
    right, left = lax.rem(t + 1, loop_size), lax.rem(t + loop_size - 1, loop_size)
    opposite = lax.rem(t + loop_size // 2, loop_size)
    innermost, outermost = shell == 0, shell == shells - 1
    inner = lax.max(shell - 1, 0)
    outer = lax.min(shell + 1, shells - 1)

    def signal(barrier, at):
        pl.semaphore_signal(barrier, inc=1, device_id=at, device_id_type=MESH)

    barrier = pltpu.get_barrier_semaphore()
    signal(barrier, (right, shell))
    signal(barrier, (left, shell))
    pl.when(innermost)(lambda: signal(barrier, (opposite, shell)))
    pl.when(jnp.logical_not(innermost))(lambda: signal(barrier, (t, inner)))
    pl.when(jnp.logical_not(outermost))(lambda: signal(barrier, (t, outer)))

    own = pltpu.make_async_copy(v, ext.at[:, pl.ds(2, width), pl.ds(PAD, rows), :], own_sem)
    own.start()

    pl.semaphore_wait(barrier, jnp.where(outermost, 3, 4))

    size = rows // PIECES
    arriving = []
    for p in range(PIECES):
        part, there = pl.ds(p * size, size), pl.ds(PAD + p * size, size)
        for d, (at, src, dst) in enumerate(((right, width - 2, 0), (left, 0, width + 2))):
            copy = pltpu.make_async_remote_copy(
                src_ref=v.at[:, pl.ds(src, 2), part, :],
                dst_ref=ext.at[:, pl.ds(dst, 2), there, :],
                send_sem=send_sem.at[d, p],
                recv_sem=recv_sem.at[d, p],
                device_id=(at, shell),
                device_id_type=MESH,
            )
            copy.start()
            arriving.append(copy)
        if p == 0:
            layers = pl.ds(2, width)
            inward = pltpu.make_async_remote_copy(
                src_ref=v.at[:, :, pl.ds(0, PAD), :],
                dst_ref=ext.at[:, layers, pl.ds(top, PAD), :],
                send_sem=ghost_send.at[0],
                recv_sem=ghost_recv.at[0],
                device_id=(t, inner),
                device_id_type=MESH,
            )
            across = pltpu.make_async_remote_copy(
                src_ref=v.at[:, :, pl.ds(0, PAD), :],
                dst_ref=ext.at[:, layers, pl.ds(0, PAD), :],
                send_sem=ghost_send.at[0],
                recv_sem=ghost_recv.at[1],
                device_id=(opposite, shell),
                device_id_type=MESH,
            )
            outward = pltpu.make_async_remote_copy(
                src_ref=v.at[:, :, pl.ds(rows - PAD, PAD), :],
                dst_ref=ext.at[:, layers, pl.ds(0, PAD), :],
                send_sem=ghost_send.at[1],
                recv_sem=ghost_recv.at[1],
                device_id=(t, outer),
                device_id_type=MESH,
            )
            pl.when(innermost)(across.start)
            pl.when(jnp.logical_not(innermost))(inward.start)
            pl.when(jnp.logical_not(outermost))(outward.start)

    blocks = rows // BLOCK

    @pl.loop(0, blocks)
    def _(b):
        row = pl.multiple_of(b * BLOCK, BLOCK)
        place = lax.broadcasted_iota(jnp.int32, (BLOCK, v.shape[3]), 0) + (shell * rows + row)
        place = place.astype(jnp.float32)
        weights[0, pl.ds(row, BLOCK), :] = 1.0 / (2.0 * place + 1.0)
        weights[1, pl.ds(row, BLOCK), :] = (place + 0.5) * (1.0 / grid_r)

    own.wait()

    @pl.loop(0, blocks)
    def _(b):
        row = pl.multiple_of(b * BLOCK, BLOCK)
        for m in range(2, width - 2):
            azimuth_block(ext, weights, azimuth, m, row, grid_r, grid_t)

    across.wait_recv()
    pl.when(jnp.logical_not(outermost))(inward.wait_recv)

    @pl.when(innermost)
    def _():
        for c, sign in enumerate((-1.0, -1.0, 1.0)):
            for m in range(2, width + 2):
                facing = ext[c, m, 0:PAD, :]
                ext[c, m, PAD - 1 : PAD, :] = facing[0:1] * sign
                ext[c, m, PAD - 2 : PAD - 1, :] = facing[1:2] * sign

    @pl.when(outermost)
    def _():
        for c in range(3):
            for m in range(2, width + 2):
                last = ext[c, m, top - PAD : top, :]
                ext[c, m, top : top + 1, :] = -last[PAD - 1 : PAD]
                ext[c, m, top + 1 : top + 2, :] = -last[PAD - 2 : PAD - 1]

    @pl.loop(0, blocks)
    def _(b):
        row = pl.multiple_of(b * BLOCK, BLOCK)

        @pl.loop(0, width)
        def _(m):
            radial_block(ext, weights, radial, m, row, grid_r)

    for p in range(PIECES):
        for d in range(2):
            arriving[2 * p + d].wait_recv()

        @pl.loop(p * (size // BLOCK), (p + 1) * (size // BLOCK))
        def _(b):
            row = pl.multiple_of(b * BLOCK, BLOCK)
            for m in (0, 1, width - 2, width - 1):
                azimuth_block(ext, weights, azimuth, m, row, grid_r, grid_t)

    for copy in arriving:
        copy.wait_send()
    inward.wait_send()
    pl.when(jnp.logical_not(outermost))(outward.wait_send)


def write_out(radial_in, azimuth_in, radial, azimuth, sems):
    copies = []
    for k, (src, dst) in enumerate(((radial_in, radial), (azimuth_in, azimuth))):
        for c in range(3):
            copies.append(pltpu.make_async_copy(src.at[c], dst.at[c], sems.at[k, c]))
    for copy in copies:
        copy.start()
    for copy in copies:
        copy.wait()


def solution(mesh):
    loop_size, shells = mesh.shape["theta"], mesh.shape["row"]

    def per_device(v):
        _, width, rows, planes = v.shape
        result = jax.ShapeDtypeStruct(v.shape, jnp.bfloat16)
        held = pltpu.VMEM(v.shape, jnp.bfloat16)
        vmem = pl.BlockSpec(memory_space=pltpu.VMEM)
        hbm = pl.BlockSpec(memory_space=pltpu.HBM)
        dma = pltpu.SemaphoreType.DMA
        radial, azimuth = pl.pallas_call(
            functools.partial(tendencies, loop_size, shells),
            out_shape=(held, held),
            in_specs=[hbm],
            out_specs=(vmem, vmem),
            scratch_shapes=[
                pltpu.VMEM((3, width + 4, rows + 2 * PAD, planes), jnp.float32),
                pltpu.VMEM((2, rows, planes), jnp.float32),
                dma,
                dma((2, PIECES)),
                dma((2, PIECES)),
                dma((2,)),
                dma((2,)),
            ],
            compiler_params=pltpu.CompilerParams(
                collective_id=0, has_side_effects=True, vmem_limit_bytes=32 << 20
            ),
        )(pltpu.with_memory_space_constraint(v, pltpu.HBM))
        radial = pltpu.with_memory_space_constraint(radial, pltpu.VMEM)
        azimuth = pltpu.with_memory_space_constraint(azimuth, pltpu.VMEM)
        return pl.pallas_call(
            write_out,
            out_shape=(result, result),
            in_specs=[vmem, vmem],
            out_specs=(hbm, hbm),
            scratch_shapes=[dma((2, 3))],
            compiler_params=pltpu.CompilerParams(vmem_limit_bytes=32 << 20),
        )(radial, azimuth)

    spec = P(None, "theta", "row", None)
    return jax.shard_map(
        per_device, mesh=mesh, in_specs=(spec,), out_specs=(spec, spec), check_vma=False
    )
```

```python
import functools
import math

import jax
import jax.numpy as jnp
from jax import lax
from jax.experimental import pallas as pl
from jax.experimental.pallas import tpu as pltpu
from jax.sharding import PartitionSpec as P

MESH = pl.DeviceIdType.MESH
PAD = 8
BLOCK = 32
RUN = 8
END = 16
PIECES = 4


def radial_block(ext, weights, out, m, row, count):
    slope_r = 0.2 / 12.0
    slope_z = 0.2 / 48.0
    lap_r = 0.1
    lap_z = 0.1 / 16.0
    mid = pl.ds(row + PAD, count)
    inverse = weights[0, pl.ds(row, count), :]
    u_rad = ext[0, m + 2, mid, :]
    u_ax = ext[2, m + 2, mid, :]
    radial_two = u_rad * (-slope_r)
    radial_one = radial_two * 8.0 + lap_r * inverse
    axial_two = u_ax * (-slope_z)
    axial_one = axial_two * 8.0
    for c in range(3):
        f = ext[c, m + 2, mid, :]
        out_one = ext[c, m + 2, pl.ds(row + PAD + 1, count), :]
        in_one = ext[c, m + 2, pl.ds(row + PAD - 1, count), :]
        out_two = ext[c, m + 2, pl.ds(row + PAD + 2, count), :]
        in_two = ext[c, m + 2, pl.ds(row + PAD - 2, count), :]
        planes = f.shape[1]
        ahead_one = pltpu.roll(f, planes - 1, 1)
        behind_one = pltpu.roll(f, 1, 1)
        ahead_two = pltpu.roll(f, planes - 2, 1)
        behind_two = pltpu.roll(f, 2, 1)
        total = (out_one - in_one) * radial_one - (out_two - in_two) * radial_two
        total += (ahead_one - behind_one) * axial_one - (ahead_two - behind_two) * axial_two
        total += (out_one + in_one) * lap_r + (ahead_one + behind_one) * lap_z
        total -= f * (2.0 * (lap_r + lap_z))
        out[c, m, pl.ds(row, count), :] = total.astype(out.dtype)


def azimuth_block(ext, weights, out, m, row, grid_r, grid_t):
    step = 2.0 * math.pi / grid_t
    angle_time = 2.0 / grid_r
    small = angle_time * 0.5 / grid_r
    lap = small / (step * step)
    slope = 8.0 / (12.0 * step)
    mid = pl.ds(row + PAD, BLOCK)
    radius = weights[1, pl.ds(row, BLOCK), :] * angle_time
    u_rad = ext[0, m + 2, mid, :]
    u_ang = ext[1, m + 2, mid, :]
    carried = radius * u_ang
    slopes, totals = [], []
    for c in range(3):
        f = u_rad if c == 0 else u_ang if c == 1 else ext[c, m + 2, mid, :]
        up = ext[c, m + 3, mid, :]
        down = ext[c, m + 1, mid, :]
        wide = ext[c, m + 4, mid, :] - ext[c, m, mid, :]
        slopes.append(((up - down) - wide * 0.125) * slope)
        totals.append((up + down) * lap - f * (2.0 * lap if c == 2 else 2.0 * lap + small))
    totals[0] += carried * (u_ang - slopes[0]) - slopes[1] * (2.0 * small)
    totals[1] += slopes[0] * (2.0 * small) - carried * (u_rad + slopes[1])
    totals[2] -= carried * slopes[2]
    for c in range(3):
        out[c, m, pl.ds(row, BLOCK), :] = totals[c].astype(out.dtype)


def tendencies(
    loop_size, shells, v, radial, azimuth, ext, weights, stage, ghost,
    own_sem, send_sem, recv_sem, ghost_send, ghost_recv, ready, turn,
):
    width, rows = v.shape[1], v.shape[2]
    grid_r, grid_t = rows * shells, width * loop_size
    top = rows + PAD
    t = lax.axis_index("theta")
    shell = lax.axis_index("row")
    right, left = lax.rem(t + 1, loop_size), lax.rem(t + loop_size - 1, loop_size)
    opposite = lax.rem(t + loop_size // 2, loop_size)
    innermost, outermost = shell == 0, shell == shells - 1
    not_innermost, not_outermost = shell > 0, shell < shells - 1
    first_half = innermost & (t < loop_size // 2)
    second_half = innermost & (t >= loop_size // 2)
    inner = lax.max(shell - 1, 0)
    outer = lax.min(shell + 1, shells - 1)

    def signal(sem, at):
        pl.semaphore_signal(sem, inc=1, device_id=at, device_id_type=MESH)

    barrier = pltpu.get_barrier_semaphore()
    signal(barrier, (left, shell))
    pl.when(not_outermost)(lambda: signal(barrier, (t, outer)))
    pl.when(first_half)(lambda: signal(barrier, (opposite, shell)))

    own = pltpu.make_async_copy(v, ext.at[:, pl.ds(2, width), pl.ds(PAD, rows), :], own_sem)
    own.start()

    partners = 1 + not_innermost.astype(jnp.int32) + second_half.astype(jnp.int32)
    pl.semaphore_wait(barrier, partners)
    signal(ready.at[0], (right, shell))
    pl.when(not_innermost)(lambda: signal(ready.at[1], (t, inner)))
    pl.when(second_half)(lambda: signal(ready.at[2], (opposite, shell)))

    size = rows // PIECES

    def layers_copy(d, p):
        at, src, dst = ((right, width - 2, 0), (left, 0, width + 2))[d]
        return pltpu.make_async_remote_copy(
            src_ref=v.at[:, pl.ds(src, 2), pl.ds(p * size, size), :],
            dst_ref=ext.at[:, pl.ds(dst, 2), pl.ds(PAD + p * size, size), :],
            send_sem=send_sem.at[d, p],
            recv_sem=recv_sem.at[d, p],
            device_id=(at, shell),
            device_id_type=MESH,
        )

    rightward = [layers_copy(0, p) for p in range(PIECES)]
    leftward = [layers_copy(1, p) for p in range(PIECES)]

    last_plane = lax.rem(t, RUN) == RUN - 1
    even = lax.rem(shell, 2) == 0
    waits_turn = last_plane & even
    gives_turn = last_plane & jnp.logical_not(even)

    @pl.when(jnp.logical_not(waits_turn))
    def _():
        for copy in rightward:
            copy.start()

    pl.semaphore_wait(ready.at[0], 1)
    for copy in leftward:
        copy.start()

    own.wait()

    for c in range(3):
        for m in range(width):
            at = 2 * (c * width + m)
            head = ext[c, m + 2, PAD : PAD + 2, :]
            across = jnp.concatenate([head[1:2], head[0:1]], axis=0) * (1.0 if c == 2 else -1.0)
            stage[0, at : at + 2, :] = jnp.where(innermost, across, head)
            stage[1, at : at + 2, :] = ext[c, m + 2, top - 2 : top, :]

    def ghost_copy(src, dst, at):
        return pltpu.make_async_remote_copy(
            src_ref=stage.at[src],
            dst_ref=ghost.at[dst],
            send_sem=ghost_send.at[src],
            recv_sem=ghost_recv.at[dst],
            device_id=at,
            device_id_type=MESH,
        )

    across = ghost_copy(0, 0, (opposite, shell))
    inward = ghost_copy(0, 1, (t, inner))
    outward = ghost_copy(1, 0, (t, outer))
    pl.when(not_innermost)(inward.start)

    @pl.when(not_outermost)
    def _():
        pl.semaphore_wait(ready.at[1], 1)
        outward.start()

    pl.when(first_half)(lambda: pl.semaphore_wait(ready.at[2], 1))
    pl.when(innermost)(across.start)

    blocks = rows // BLOCK

    @pl.loop(0, blocks)
    def _(b):
        row = pl.multiple_of(b * BLOCK, BLOCK)
        place = lax.broadcasted_iota(jnp.int32, (BLOCK, v.shape[3]), 0) + (shell * rows + row)
        place = place.astype(jnp.float32)
        weights[0, pl.ds(row, BLOCK), :] = 1.0 / (2.0 * place + 1.0)
        weights[1, pl.ds(row, BLOCK), :] = (place + 0.5) * (1.0 / grid_r)

    @pl.loop(0, blocks)
    def _(b):
        row = pl.multiple_of(b * BLOCK, BLOCK)
        for m in range(2, width - 2):
            azimuth_block(ext, weights, azimuth, m, row, grid_r, grid_t)

    half = rows // 2 - END

    @pl.loop(0, width)
    def _(m):
        radial_block(ext, weights, radial, m, END, half)
        radial_block(ext, weights, radial, m, END + half, half)

    @pl.when(gives_turn)
    def _():
        for copy in rightward:
            copy.wait_send()
        signal(turn, (t, inner))

    @pl.when(waits_turn)
    def _():
        pl.semaphore_wait(turn, 1)
        for copy in rightward:
            copy.start()

    def edge_piece(copy, m, p):
        copy.wait_recv()

        @pl.loop(p * (size // BLOCK), (p + 1) * (size // BLOCK))
        def _(b):
            row = pl.multiple_of(b * BLOCK, BLOCK)
            azimuth_block(ext, weights, azimuth, m, row, grid_r, grid_t)
            azimuth_block(ext, weights, azimuth, m + 1, row, grid_r, grid_t)

    for p in range(PIECES):
        edge_piece(leftward[p], width - 2, p)

    across.wait_recv()
    pl.when(not_outermost)(inward.wait_recv)
    for c in range(3):
        for m in range(width):
            at = 2 * (c * width + m)
            ext[c, m + 2, PAD - 2 : PAD, :] = ghost[0, at : at + 2, :]
            last = ext[c, m + 2, top - 2 : top, :]
            wall = jnp.concatenate([last[1:2], last[0:1]], axis=0) * -1.0
            ext[c, m + 2, top : top + 2, :] = jnp.where(outermost, wall, ghost[1, at : at + 2, :])

    @pl.loop(0, width // 2)
    def _(k):
        for m in (2 * k, 2 * k + 1):
            radial_block(ext, weights, radial, m, 0, END)
            radial_block(ext, weights, radial, m, rows - END, END)

    for p in range(PIECES):
        edge_piece(rightward[p], 0, p)

    for copy in leftward:
        copy.wait_send()

    @pl.when(jnp.logical_not(gives_turn))
    def _():
        for copy in rightward:
            copy.wait_send()

    inward.wait_send()
    pl.when(not_outermost)(outward.wait_send)


def write_out(radial_in, azimuth_in, radial, azimuth, sems):
    copies = []
    for k, (src, dst) in enumerate(((radial_in, radial), (azimuth_in, azimuth))):
        for c in range(3):
            copies.append(pltpu.make_async_copy(src.at[c], dst.at[c], sems.at[k, c]))
    for copy in copies:
        copy.start()
    for copy in copies:
        copy.wait()


def solution(mesh):
    loop_size, shells = mesh.shape["theta"], mesh.shape["row"]

    def per_device(v):
        _, width, rows, planes = v.shape
        result = jax.ShapeDtypeStruct(v.shape, jnp.bfloat16)
        held = pltpu.VMEM(v.shape, jnp.bfloat16)
        vmem = pl.BlockSpec(memory_space=pltpu.VMEM)
        hbm = pl.BlockSpec(memory_space=pltpu.HBM)
        dma = pltpu.SemaphoreType.DMA
        radial, azimuth = pl.pallas_call(
            functools.partial(tendencies, loop_size, shells),
            out_shape=(held, held),
            in_specs=[hbm],
            out_specs=(vmem, vmem),
            scratch_shapes=[
                pltpu.VMEM((3, width + 4, rows + 2 * PAD, planes), jnp.float32),
                pltpu.VMEM((2, rows, planes), jnp.float32),
                pltpu.VMEM((2, 6 * width, planes), jnp.float32),
                pltpu.VMEM((2, 6 * width, planes), jnp.float32),
                dma,
                dma((2, PIECES)),
                dma((2, PIECES)),
                dma((2,)),
                dma((2,)),
                pltpu.SemaphoreType.REGULAR((3,)),
                pltpu.SemaphoreType.REGULAR,
            ],
            compiler_params=pltpu.CompilerParams(
                collective_id=0, has_side_effects=True, vmem_limit_bytes=32 << 20
            ),
        )(pltpu.with_memory_space_constraint(v, pltpu.HBM))
        radial = pltpu.with_memory_space_constraint(radial, pltpu.VMEM)
        azimuth = pltpu.with_memory_space_constraint(azimuth, pltpu.VMEM)
        return pl.pallas_call(
            write_out,
            out_shape=(result, result),
            in_specs=[vmem, vmem],
            out_specs=(hbm, hbm),
            scratch_shapes=[dma((2, 3))],
            compiler_params=pltpu.CompilerParams(vmem_limit_bytes=32 << 20),
        )(radial, azimuth)

    spec = P(None, "theta", "row", None)
    return jax.shard_map(
        per_device, mesh=mesh, in_specs=(spec,), out_specs=(spec, spec), check_vma=False
    )
```

```python
import functools
import math

import jax
import jax.numpy as jnp
from jax import lax
from jax.experimental import pallas as pl
from jax.experimental.pallas import tpu as pltpu
from jax.sharding import PartitionSpec as P

MESH = pl.DeviceIdType.MESH
PAD = 8
BLOCK = 32
RUN = 8
END = 16
PIECES = 4


def radial_block(ext, weights, out, m, row, count):
    slope_r = 0.2 / 12.0
    slope_z = 0.2 / 48.0
    lap_r = 0.1
    lap_z = 0.1 / 16.0
    mid = pl.ds(row + PAD, count)
    inverse = weights[0, pl.ds(row, count), :]
    u_rad = ext[0, m + 2, mid, :]
    u_ax = ext[2, m + 2, mid, :]
    radial_two = u_rad * (-slope_r)
    radial_one = radial_two * 8.0 + lap_r * inverse
    axial_two = u_ax * (-slope_z)
    axial_one = axial_two * 8.0
    for c in range(3):
        f = ext[c, m + 2, mid, :]
        out_one = ext[c, m + 2, pl.ds(row + PAD + 1, count), :]
        in_one = ext[c, m + 2, pl.ds(row + PAD - 1, count), :]
        out_two = ext[c, m + 2, pl.ds(row + PAD + 2, count), :]
        in_two = ext[c, m + 2, pl.ds(row + PAD - 2, count), :]
        planes = f.shape[1]
        ahead_one = pltpu.roll(f, planes - 1, 1)
        behind_one = pltpu.roll(f, 1, 1)
        ahead_two = pltpu.roll(f, planes - 2, 1)
        behind_two = pltpu.roll(f, 2, 1)
        total = (out_one - in_one) * radial_one - (out_two - in_two) * radial_two
        total += (ahead_one - behind_one) * axial_one - (ahead_two - behind_two) * axial_two
        total += (out_one + in_one) * lap_r + (ahead_one + behind_one) * lap_z
        total -= f * (2.0 * (lap_r + lap_z))
        out[c, m, pl.ds(row, count), :] = total.astype(out.dtype)


def azimuth_block(ext, weights, out, m, row, grid_r, grid_t):
    step = 2.0 * math.pi / grid_t
    angle_time = 2.0 / grid_r
    small = angle_time * 0.5 / grid_r
    lap = small / (step * step)
    slope = 8.0 / (12.0 * step)
    mid = pl.ds(row + PAD, BLOCK)
    radius = weights[1, pl.ds(row, BLOCK), :] * angle_time
    u_rad = ext[0, m + 2, mid, :]
    u_ang = ext[1, m + 2, mid, :]
    carried = radius * u_ang
    slopes, totals = [], []
    for c in range(3):
        f = u_rad if c == 0 else u_ang if c == 1 else ext[c, m + 2, mid, :]
        up = ext[c, m + 3, mid, :]
        down = ext[c, m + 1, mid, :]
        wide = ext[c, m + 4, mid, :] - ext[c, m, mid, :]
        slopes.append(((up - down) - wide * 0.125) * slope)
        totals.append((up + down) * lap - f * (2.0 * lap if c == 2 else 2.0 * lap + small))
    totals[0] += carried * (u_ang - slopes[0]) - slopes[1] * (2.0 * small)
    totals[1] += slopes[0] * (2.0 * small) - carried * (u_rad + slopes[1])
    totals[2] -= carried * slopes[2]
    for c in range(3):
        out[c, m, pl.ds(row, BLOCK), :] = totals[c].astype(out.dtype)


def tendencies(
    loop_size, shells, v, radial, azimuth, ext, weights, stage, ghost,
    own_sem, send_sem, recv_sem, ghost_send, ghost_recv, ready,
):
    width, rows = v.shape[1], v.shape[2]
    grid_r, grid_t = rows * shells, width * loop_size
    top = rows + PAD
    t = lax.axis_index("theta")
    shell = lax.axis_index("row")
    right, left = lax.rem(t + 1, loop_size), lax.rem(t + loop_size - 1, loop_size)
    opposite = lax.rem(t + loop_size // 2, loop_size)
    innermost, outermost = shell == 0, shell == shells - 1
    not_innermost, not_outermost = shell > 0, shell < shells - 1
    first_half = innermost & (t < loop_size // 2)
    second_half = innermost & (t >= loop_size // 2)
    inner = lax.max(shell - 1, 0)
    outer = lax.min(shell + 1, shells - 1)

    def signal(sem, at):
        pl.semaphore_signal(sem, inc=1, device_id=at, device_id_type=MESH)

    odd = lax.rem(shell, 2) == 1
    even = jnp.logical_not(odd)
    barrier = pltpu.get_barrier_semaphore()
    signal(barrier, (left, shell))
    pl.when(odd)(lambda: signal(barrier, (t, inner)))
    pl.when(odd & not_outermost)(lambda: signal(barrier, (t, outer)))
    pl.when(first_half)(lambda: signal(barrier, (opposite, shell)))

    own = pltpu.make_async_copy(v, ext.at[:, pl.ds(2, width), pl.ds(PAD, rows), :], own_sem)

    even_inner, even_outer = even & not_innermost, even & not_outermost
    partners = 1 + even_inner.astype(jnp.int32) + even_outer.astype(jnp.int32) + second_half.astype(jnp.int32)
    pl.semaphore_wait(barrier, partners)

    size = rows // PIECES

    def layers_copy(d, p):
        at, src, dst = ((right, width - 2, 0), (left, 0, width + 2))[d]
        return pltpu.make_async_remote_copy(
            src_ref=v.at[:, pl.ds(src, 2), pl.ds(p * size, size), :],
            dst_ref=ext.at[:, pl.ds(dst, 2), pl.ds(PAD + p * size, size), :],
            send_sem=send_sem.at[d, p],
            recv_sem=recv_sem.at[d, p],
            device_id=(at, shell),
            device_id_type=MESH,
        )

    rightward = [layers_copy(0, p) for p in range(PIECES)]
    leftward = [layers_copy(1, p) for p in range(PIECES)]

    for copy in rightward:
        copy.start()
    signal(ready.at[0], (right, shell))
    pl.when(even_inner)(lambda: signal(ready.at[1], (t, inner)))
    pl.when(even_outer)(lambda: signal(ready.at[3], (t, outer)))
    pl.when(second_half)(lambda: signal(ready.at[2], (opposite, shell)))
    own.start()

    first_plane = lax.rem(t, RUN) == 0

    def send_leftward():
        pl.semaphore_wait(ready.at[0], 1)
        for copy in leftward:
            copy.start()

    pl.when(jnp.logical_not(first_plane))(send_leftward)

    own.wait()

    for c in range(3):
        for m in range(width):
            at = 2 * (c * width + m)
            head = ext[c, m + 2, PAD : PAD + 2, :]
            across = jnp.concatenate([head[1:2], head[0:1]], axis=0) * (1.0 if c == 2 else -1.0)
            stage[0, at : at + 2, :] = jnp.where(innermost, across, head)
            stage[1, at : at + 2, :] = ext[c, m + 2, top - 2 : top, :]

    def ghost_copy(src, dst, at):
        return pltpu.make_async_remote_copy(
            src_ref=stage.at[src],
            dst_ref=ghost.at[dst],
            send_sem=ghost_send.at[src],
            recv_sem=ghost_recv.at[dst],
            device_id=at,
            device_id_type=MESH,
        )

    across = ghost_copy(0, 0, (opposite, shell))
    inward = ghost_copy(0, 1, (t, inner))
    outward = ghost_copy(1, 0, (t, outer))
    pl.when(odd)(lambda: pl.semaphore_wait(ready.at[3], 1))
    pl.when(not_innermost)(inward.start)
    pl.when(odd & not_outermost)(lambda: pl.semaphore_wait(ready.at[1], 1))
    pl.when(not_outermost)(outward.start)

    pl.when(first_half)(lambda: pl.semaphore_wait(ready.at[2], 1))
    pl.when(innermost)(across.start)

    pl.when(first_plane)(send_leftward)

    blocks = rows // BLOCK

    @pl.loop(0, blocks)
    def _(b):
        row = pl.multiple_of(b * BLOCK, BLOCK)
        place = lax.broadcasted_iota(jnp.int32, (BLOCK, v.shape[3]), 0) + (shell * rows + row)
        place = place.astype(jnp.float32)
        weights[0, pl.ds(row, BLOCK), :] = 1.0 / (2.0 * place + 1.0)
        weights[1, pl.ds(row, BLOCK), :] = (place + 0.5) * (1.0 / grid_r)

    @pl.loop(0, blocks)
    def _(b):
        row = pl.multiple_of(b * BLOCK, BLOCK)
        for m in range(2, width - 2):
            azimuth_block(ext, weights, azimuth, m, row, grid_r, grid_t)

    half = rows // 2 - END

    @pl.loop(0, width)
    def _(m):
        radial_block(ext, weights, radial, m, END, half)
        radial_block(ext, weights, radial, m, END + half, half)

    across.wait_recv()
    pl.when(not_outermost)(inward.wait_recv)
    for c in range(3):
        for m in range(width):
            at = 2 * (c * width + m)
            ext[c, m + 2, PAD - 2 : PAD, :] = ghost[0, at : at + 2, :]
            last = ext[c, m + 2, top - 2 : top, :]
            wall = jnp.concatenate([last[1:2], last[0:1]], axis=0) * -1.0
            ext[c, m + 2, top : top + 2, :] = jnp.where(outermost, wall, ghost[1, at : at + 2, :])

    @pl.loop(0, width // 2)
    def _(k):
        for m in (2 * k, 2 * k + 1):
            radial_block(ext, weights, radial, m, 0, END)
            radial_block(ext, weights, radial, m, rows - END, END)

    def edge_piece(copy, m, p):
        copy.wait_recv()

        @pl.loop(p * (size // BLOCK), (p + 1) * (size // BLOCK))
        def _(b):
            row = pl.multiple_of(b * BLOCK, BLOCK)
            azimuth_block(ext, weights, azimuth, m, row, grid_r, grid_t)
            azimuth_block(ext, weights, azimuth, m + 1, row, grid_r, grid_t)

    for p in range(PIECES):
        edge_piece(leftward[p], width - 2, p)

    for p in range(PIECES):
        edge_piece(rightward[p], 0, p)

    for copy in rightward + leftward:
        copy.wait_send()
    inward.wait_send()
    pl.when(not_outermost)(outward.wait_send)


def write_out(radial_in, azimuth_in, radial, azimuth, sems):
    copies = []
    for k, (src, dst) in enumerate(((radial_in, radial), (azimuth_in, azimuth))):
        for c in range(3):
            copies.append(pltpu.make_async_copy(src.at[c], dst.at[c], sems.at[k, c]))
    for copy in copies:
        copy.start()
    for copy in copies:
        copy.wait()


def solution(mesh):
    loop_size, shells = mesh.shape["theta"], mesh.shape["row"]

    def per_device(v):
        _, width, rows, planes = v.shape
        result = jax.ShapeDtypeStruct(v.shape, jnp.bfloat16)
        held = pltpu.VMEM(v.shape, jnp.bfloat16)
        vmem = pl.BlockSpec(memory_space=pltpu.VMEM)
        hbm = pl.BlockSpec(memory_space=pltpu.HBM)
        dma = pltpu.SemaphoreType.DMA
        radial, azimuth = pl.pallas_call(
            functools.partial(tendencies, loop_size, shells),
            out_shape=(held, held),
            in_specs=[hbm],
            out_specs=(vmem, vmem),
            scratch_shapes=[
                pltpu.VMEM((3, width + 4, rows + 2 * PAD, planes), jnp.float32),
                pltpu.VMEM((2, rows, planes), jnp.float32),
                pltpu.VMEM((2, 6 * width, planes), jnp.float32),
                pltpu.VMEM((2, 6 * width, planes), jnp.float32),
                dma,
                dma((2, PIECES)),
                dma((2, PIECES)),
                dma((2,)),
                dma((2,)),
                pltpu.SemaphoreType.REGULAR((4,)),
            ],
            compiler_params=pltpu.CompilerParams(
                collective_id=0, has_side_effects=True, vmem_limit_bytes=32 << 20
            ),
        )(pltpu.with_memory_space_constraint(v, pltpu.HBM))
        radial = pltpu.with_memory_space_constraint(radial, pltpu.VMEM)
        azimuth = pltpu.with_memory_space_constraint(azimuth, pltpu.VMEM)
        return pl.pallas_call(
            write_out,
            out_shape=(result, result),
            in_specs=[vmem, vmem],
            out_specs=(hbm, hbm),
            scratch_shapes=[dma((2, 3))],
            compiler_params=pltpu.CompilerParams(vmem_limit_bytes=32 << 20),
        )(radial, azimuth)

    spec = P(None, "theta", "row", None)
    return jax.shard_map(
        per_device, mesh=mesh, in_specs=(spec,), out_specs=(spec, spec), check_vma=False
    )
```

```python
import functools
import math

import jax
import jax.numpy as jnp
from jax import lax
from jax.experimental import pallas as pl
from jax.experimental.pallas import tpu as pltpu
from jax.sharding import PartitionSpec as P

MESH = pl.DeviceIdType.MESH
PAD = 8
BLOCK = 32
RUN = 8
PLANE = 32
RELAY = 7
SHARE = 16
END = 16
PIECES = 4


def radial_block(ext, weights, out, m, row, count):
    slope_r = 0.2 / 12.0
    slope_z = 0.2 / 48.0
    lap_r = 0.1
    lap_z = 0.1 / 16.0
    mid = pl.ds(row + PAD, count)
    inverse = weights[0, pl.ds(row, count), :]
    u_rad = ext[0, m + 2, mid, :]
    u_ax = ext[2, m + 2, mid, :]
    radial_two = u_rad * (-slope_r)
    radial_one = radial_two * 8.0 + lap_r * inverse
    axial_two = u_ax * (-slope_z)
    axial_one = axial_two * 8.0
    for c in range(3):
        f = ext[c, m + 2, mid, :]
        out_one = ext[c, m + 2, pl.ds(row + PAD + 1, count), :]
        in_one = ext[c, m + 2, pl.ds(row + PAD - 1, count), :]
        out_two = ext[c, m + 2, pl.ds(row + PAD + 2, count), :]
        in_two = ext[c, m + 2, pl.ds(row + PAD - 2, count), :]
        planes = f.shape[1]
        ahead_one = pltpu.roll(f, planes - 1, 1)
        behind_one = pltpu.roll(f, 1, 1)
        ahead_two = pltpu.roll(f, planes - 2, 1)
        behind_two = pltpu.roll(f, 2, 1)
        total = (out_one - in_one) * radial_one - (out_two - in_two) * radial_two
        total += (ahead_one - behind_one) * axial_one - (ahead_two - behind_two) * axial_two
        total += (out_one + in_one) * lap_r + (ahead_one + behind_one) * lap_z
        total -= f * (2.0 * (lap_r + lap_z))
        out[c, m, pl.ds(row, count), :] = total.astype(out.dtype)


def azimuth_block(ext, weights, out, m, row, grid_r, grid_t):
    step = 2.0 * math.pi / grid_t
    angle_time = 2.0 / grid_r
    small = angle_time * 0.5 / grid_r
    lap = small / (step * step)
    slope = 8.0 / (12.0 * step)
    mid = pl.ds(row + PAD, BLOCK)
    radius = weights[1, pl.ds(row, BLOCK), :] * angle_time
    u_rad = ext[0, m + 2, mid, :]
    u_ang = ext[1, m + 2, mid, :]
    carried = radius * u_ang
    slopes, totals = [], []
    for c in range(3):
        f = u_rad if c == 0 else u_ang if c == 1 else ext[c, m + 2, mid, :]
        up = ext[c, m + 3, mid, :]
        down = ext[c, m + 1, mid, :]
        wide = ext[c, m + 4, mid, :] - ext[c, m, mid, :]
        slopes.append(((up - down) - wide * 0.125) * slope)
        totals.append((up + down) * lap - f * (2.0 * lap if c == 2 else 2.0 * lap + small))
    totals[0] += carried * (u_ang - slopes[0]) - slopes[1] * (2.0 * small)
    totals[1] += slopes[0] * (2.0 * small) - carried * (u_rad + slopes[1])
    totals[2] -= carried * slopes[2]
    for c in range(3):
        out[c, m, pl.ds(row, BLOCK), :] = totals[c].astype(out.dtype)


def tendencies(
    loop_size, shells, v, radial, azimuth, ext, weights, stage, ghost,
    own_sem, send_sem, recv_sem, ghost_send, ghost_recv, ready, passing, passing_ready, relay_send, relay_recv,
):
    width, rows = v.shape[1], v.shape[2]
    grid_r, grid_t = rows * shells, width * loop_size
    top = rows + PAD
    t = lax.axis_index("theta")
    shell = lax.axis_index("row")
    right, left = lax.rem(t + 1, loop_size), lax.rem(t + loop_size - 1, loop_size)
    opposite = lax.rem(t + loop_size // 2, loop_size)
    innermost, outermost = shell == 0, shell == shells - 1
    not_innermost, not_outermost = shell > 0, shell < shells - 1
    first_half = innermost & (t < loop_size // 2)
    second_half = innermost & (t >= loop_size // 2)
    inner = lax.max(shell - 1, 0)
    outer = lax.min(shell + 1, shells - 1)

    def signal(sem, at):
        pl.semaphore_signal(sem, inc=1, device_id=at, device_id_type=MESH)

    odd = lax.rem(shell, 2) == 1
    even = jnp.logical_not(odd)
    barrier = pltpu.get_barrier_semaphore()
    signal(barrier, (left, shell))
    pl.when(odd)(lambda: signal(barrier, (t, inner)))
    pl.when(odd & not_outermost)(lambda: signal(barrier, (t, outer)))
    pl.when(first_half)(lambda: signal(barrier, (opposite, shell)))

    place = lax.rem(t, PLANE)
    sender, receiver, relay = place == PLANE - 1, place == 0, place == RELAY
    received_from, relayed_to = lax.rem(right + RELAY, loop_size), lax.max(t - RELAY, 0)
    pl.when(receiver)(lambda: signal(barrier, (lax.rem(t + RELAY, loop_size), shell)))

    own = pltpu.make_async_copy(v, ext.at[:, pl.ds(2, width), pl.ds(PAD, rows), :], own_sem)

    even_inner, even_outer = even & not_innermost, even & not_outermost
    partners = 1 + even_inner.astype(jnp.int32) + even_outer.astype(jnp.int32) + second_half.astype(jnp.int32)
    partners += relay.astype(jnp.int32)
    pl.semaphore_wait(barrier, partners)

    size = rows // PIECES
    tail = rows - SHARE
    leftward_rows = [(p * size, size) for p in range(PIECES)]
    rightward_rows = [(tail, SHARE)] + [(p * size, min(size, tail - p * size)) for p in range(PIECES)]

    def layers_copy(d, p, start, count):
        at, src, dst = ((right, width - 2, 0), (left, 0, width + 2))[d]
        return pltpu.make_async_remote_copy(
            src_ref=v.at[:, pl.ds(src, 2), pl.ds(start, count), :],
            dst_ref=ext.at[:, pl.ds(dst, 2), pl.ds(PAD + start, count), :],
            send_sem=send_sem.at[d, p],
            recv_sem=recv_sem.at[d, p],
            device_id=(at, shell),
            device_id_type=MESH,
        )

    rightward = [layers_copy(0, p, *part) for p, part in enumerate(rightward_rows)]
    leftward = [layers_copy(1, p, *part) for p, part in enumerate(leftward_rows)]

    pl.when(jnp.logical_not(sender))(rightward[0].start)
    for copy in rightward[1:]:
        copy.start()
    signal(ready.at[0], (right, shell))
    pl.when(even_inner)(lambda: signal(ready.at[1], (t, inner)))
    pl.when(even_outer)(lambda: signal(ready.at[3], (t, outer)))
    pl.when(second_half)(lambda: signal(ready.at[2], (opposite, shell)))
    pl.when(relay)(lambda: signal(passing_ready.at[0], (relayed_to, shell)))
    own.start()

    first_plane = lax.rem(t, RUN) == 0

    def send_leftward():
        pl.semaphore_wait(ready.at[0], 1)
        for copy in leftward:
            copy.start()

    pl.when(jnp.logical_not(first_plane))(send_leftward)

    own.wait()

    for c in range(3):
        for m in range(width):
            at = 2 * (c * width + m)
            head = ext[c, m + 2, PAD : PAD + 2, :]
            across = jnp.concatenate([head[1:2], head[0:1]], axis=0) * (1.0 if c == 2 else -1.0)
            stage[0, at : at + 2, :] = jnp.where(innermost, across, head)
            stage[1, at : at + 2, :] = ext[c, m + 2, top - 2 : top, :]

    def ghost_copy(src, dst, at):
        return pltpu.make_async_remote_copy(
            src_ref=stage.at[src],
            dst_ref=ghost.at[dst],
            send_sem=ghost_send.at[src],
            recv_sem=ghost_recv.at[dst],
            device_id=at,
            device_id_type=MESH,
        )

    across = ghost_copy(0, 0, (opposite, shell))
    inward = ghost_copy(0, 1, (t, inner))
    outward = ghost_copy(1, 0, (t, outer))
    pl.when(odd)(lambda: pl.semaphore_wait(ready.at[3], 1))
    pl.when(not_innermost)(inward.start)
    pl.when(odd & not_outermost)(lambda: pl.semaphore_wait(ready.at[1], 1))
    pl.when(not_outermost)(outward.start)

    pl.when(first_half)(lambda: pl.semaphore_wait(ready.at[2], 1))
    pl.when(innermost)(across.start)

    pl.when(first_plane)(send_leftward)

    @pl.when(receiver)
    def _():
        pl.semaphore_wait(passing_ready.at[0], 1)
        signal(passing_ready.at[1], (left, shell))


    blocks = rows // BLOCK

    @pl.loop(0, blocks)
    def _(b):
        row = pl.multiple_of(b * BLOCK, BLOCK)
        place = lax.broadcasted_iota(jnp.int32, (BLOCK, v.shape[3]), 0) + (shell * rows + row)
        place = place.astype(jnp.float32)
        weights[0, pl.ds(row, BLOCK), :] = 1.0 / (2.0 * place + 1.0)
        weights[1, pl.ds(row, BLOCK), :] = (place + 0.5) * (1.0 / grid_r)

    @pl.loop(0, blocks)
    def _(b):
        row = pl.multiple_of(b * BLOCK, BLOCK)
        for m in range(2, width - 2):
            azimuth_block(ext, weights, azimuth, m, row, grid_r, grid_t)

    to_relay = pltpu.make_async_remote_copy(
        src_ref=v.at[:, pl.ds(width - 2, 2), pl.ds(tail, SHARE), :],
        dst_ref=passing,
        send_sem=send_sem.at[0, 0],
        recv_sem=relay_recv,
        device_id=(received_from, shell),
        device_id_type=MESH,
    )
    from_relay = pltpu.make_async_remote_copy(
        src_ref=passing,
        dst_ref=ext.at[:, pl.ds(0, 2), pl.ds(PAD + tail, SHARE), :],
        send_sem=relay_send,
        recv_sem=recv_sem.at[0, 0],
        device_id=(relayed_to, shell),
        device_id_type=MESH,
    )

    @pl.when(sender)
    def _():
        pl.semaphore_wait(passing_ready.at[1], 1)
        to_relay.start()

    half = rows // 2 - END

    @pl.loop(0, width)
    def _(m):
        radial_block(ext, weights, radial, m, END, half)
        radial_block(ext, weights, radial, m, END + half, half)

    @pl.when(relay)
    def _():
        to_relay.wait_recv()
        from_relay.start()

    across.wait_recv()
    pl.when(not_outermost)(inward.wait_recv)
    for c in range(3):
        for m in range(width):
            at = 2 * (c * width + m)
            ext[c, m + 2, PAD - 2 : PAD, :] = ghost[0, at : at + 2, :]
            last = ext[c, m + 2, top - 2 : top, :]
            wall = jnp.concatenate([last[1:2], last[0:1]], axis=0) * -1.0
            ext[c, m + 2, top : top + 2, :] = jnp.where(outermost, wall, ghost[1, at : at + 2, :])

    @pl.loop(0, width // 2)
    def _(k):
        for m in (2 * k, 2 * k + 1):
            radial_block(ext, weights, radial, m, 0, END)
            radial_block(ext, weights, radial, m, rows - END, END)

    def edge_rows(m, start, count):
        @pl.loop(start // BLOCK, (start + count) // BLOCK)
        def _(b):
            row = pl.multiple_of(b * BLOCK, BLOCK)
            azimuth_block(ext, weights, azimuth, m, row, grid_r, grid_t)
            azimuth_block(ext, weights, azimuth, m + 1, row, grid_r, grid_t)

    for copy, part in zip(leftward, leftward_rows):
        copy.wait_recv()
        edge_rows(width - 2, *part)

    rightward[0].wait_recv()
    for copy, part in zip(rightward[1:], rightward_rows[1:]):
        copy.wait_recv()
        edge_rows(0, part[0], size)

    pl.when(relay)(from_relay.wait_send)
    for copy in rightward + leftward:
        copy.wait_send()
    inward.wait_send()
    pl.when(not_outermost)(outward.wait_send)


def write_out(radial_in, azimuth_in, radial, azimuth, sems):
    copies = []
    for k, (src, dst) in enumerate(((radial_in, radial), (azimuth_in, azimuth))):
        for c in range(3):
            copies.append(pltpu.make_async_copy(src.at[c], dst.at[c], sems.at[k, c]))
    for copy in copies:
        copy.start()
    for copy in copies:
        copy.wait()


def solution(mesh):
    loop_size, shells = mesh.shape["theta"], mesh.shape["row"]

    def per_device(v):
        _, width, rows, planes = v.shape
        result = jax.ShapeDtypeStruct(v.shape, jnp.bfloat16)
        held = pltpu.VMEM(v.shape, jnp.bfloat16)
        vmem = pl.BlockSpec(memory_space=pltpu.VMEM)
        hbm = pl.BlockSpec(memory_space=pltpu.HBM)
        dma = pltpu.SemaphoreType.DMA
        radial, azimuth = pl.pallas_call(
            functools.partial(tendencies, loop_size, shells),
            out_shape=(held, held),
            in_specs=[hbm],
            out_specs=(vmem, vmem),
            scratch_shapes=[
                pltpu.VMEM((3, width + 4, rows + 2 * PAD, planes), jnp.float32),
                pltpu.VMEM((2, rows, planes), jnp.float32),
                pltpu.VMEM((2, 6 * width, planes), jnp.float32),
                pltpu.VMEM((2, 6 * width, planes), jnp.float32),
                dma,
                dma((2, PIECES + 1)),
                dma((2, PIECES + 1)),
                dma((2,)),
                dma((2,)),
                pltpu.SemaphoreType.REGULAR((4,)),
                pltpu.VMEM((3, 2, SHARE, planes), jnp.float32),
                pltpu.SemaphoreType.REGULAR((2,)),
                dma,
                dma,
            ],
            compiler_params=pltpu.CompilerParams(
                collective_id=0, has_side_effects=True, vmem_limit_bytes=32 << 20
            ),
        )(pltpu.with_memory_space_constraint(v, pltpu.HBM))
        radial = pltpu.with_memory_space_constraint(radial, pltpu.VMEM)
        azimuth = pltpu.with_memory_space_constraint(azimuth, pltpu.VMEM)
        return pl.pallas_call(
            write_out,
            out_shape=(result, result),
            in_specs=[vmem, vmem],
            out_specs=(hbm, hbm),
            scratch_shapes=[dma((2, 3))],
            compiler_params=pltpu.CompilerParams(vmem_limit_bytes=32 << 20),
        )(radial, azimuth)

    spec = P(None, "theta", "row", None)
    return jax.shard_map(
        per_device, mesh=mesh, in_specs=(spec,), out_specs=(spec, spec), check_vma=False
    )
```

```python
import functools
import math

import jax
import jax.numpy as jnp
from jax import lax
from jax.experimental import pallas as pl
from jax.experimental.pallas import tpu as pltpu
from jax.sharding import PartitionSpec as P

MESH = pl.DeviceIdType.MESH
PAD = 8
BLOCK = 32
RUN = 8
PLANE = 32
RELAYS = (7,)
BACK = 24
SHARE = 24
BACK_SHARE = 24
EARLY = 2
END = 16
PIECES = 4


def radial_block(ext, weights, out, m, row, count):
    slope_r = 0.2 / 12.0
    slope_z = 0.2 / 48.0
    lap_r = 0.1
    lap_z = 0.1 / 16.0
    mid = pl.ds(row + PAD, count)
    inverse = weights[0, pl.ds(row, count), :]
    u_rad = ext[0, m + 2, mid, :]
    u_ax = ext[2, m + 2, mid, :]
    radial_two = u_rad * (-slope_r)
    radial_one = radial_two * 8.0 + lap_r * inverse
    axial_two = u_ax * (-slope_z)
    axial_one = axial_two * 8.0
    for c in range(3):
        f = ext[c, m + 2, mid, :]
        out_one = ext[c, m + 2, pl.ds(row + PAD + 1, count), :]
        in_one = ext[c, m + 2, pl.ds(row + PAD - 1, count), :]
        out_two = ext[c, m + 2, pl.ds(row + PAD + 2, count), :]
        in_two = ext[c, m + 2, pl.ds(row + PAD - 2, count), :]
        planes = f.shape[1]
        ahead_one = pltpu.roll(f, planes - 1, 1)
        behind_one = pltpu.roll(f, 1, 1)
        ahead_two = pltpu.roll(f, planes - 2, 1)
        behind_two = pltpu.roll(f, 2, 1)
        total = (out_one - in_one) * radial_one - (out_two - in_two) * radial_two
        total += (ahead_one - behind_one) * axial_one - (ahead_two - behind_two) * axial_two
        total += (out_one + in_one) * lap_r + (ahead_one + behind_one) * lap_z
        total -= f * (2.0 * (lap_r + lap_z))
        out[c, m, pl.ds(row, count), :] = total.astype(out.dtype)


def azimuth_block(ext, weights, out, m, row, grid_r, grid_t):
    step = 2.0 * math.pi / grid_t
    angle_time = 2.0 / grid_r
    small = angle_time * 0.5 / grid_r
    lap = small / (step * step)
    slope = 8.0 / (12.0 * step)
    mid = pl.ds(row + PAD, BLOCK)
    radius = weights[1, pl.ds(row, BLOCK), :] * angle_time
    u_rad = ext[0, m + 2, mid, :]
    u_ang = ext[1, m + 2, mid, :]
    carried = radius * u_ang
    slopes, totals = [], []
    for c in range(3):
        f = u_rad if c == 0 else u_ang if c == 1 else ext[c, m + 2, mid, :]
        up = ext[c, m + 3, mid, :]
        down = ext[c, m + 1, mid, :]
        wide = ext[c, m + 4, mid, :] - ext[c, m, mid, :]
        slopes.append(((up - down) - wide * 0.125) * slope)
        totals.append((up + down) * lap - f * (2.0 * lap if c == 2 else 2.0 * lap + small))
    totals[0] += carried * (u_ang - slopes[0]) - slopes[1] * (2.0 * small)
    totals[1] += slopes[0] * (2.0 * small) - carried * (u_rad + slopes[1])
    totals[2] -= carried * slopes[2]
    for c in range(3):
        out[c, m, pl.ds(row, BLOCK), :] = totals[c].astype(out.dtype)


def tendencies(
    loop_size, shells, v, radial, azimuth, ext, weights, stage, ghost,
    own_sem, send_sem, recv_sem, ghost_send, ghost_recv, ready, passing, passing_ready, back_ready, relay_send, relay_recv,
):
    width, rows = v.shape[1], v.shape[2]
    grid_r, grid_t = rows * shells, width * loop_size
    top = rows + PAD
    t = lax.axis_index("theta")
    shell = lax.axis_index("row")
    right, left = lax.rem(t + 1, loop_size), lax.rem(t + loop_size - 1, loop_size)
    opposite = lax.rem(t + loop_size // 2, loop_size)
    innermost, outermost = shell == 0, shell == shells - 1
    not_innermost, not_outermost = shell > 0, shell < shells - 1
    first_half = innermost & (t < loop_size // 2)
    second_half = innermost & (t >= loop_size // 2)
    inner = lax.max(shell - 1, 0)
    outer = lax.min(shell + 1, shells - 1)

    def signal(sem, at):
        pl.semaphore_signal(sem, inc=1, device_id=at, device_id_type=MESH)

    odd = lax.rem(shell, 2) == 1
    even = jnp.logical_not(odd)
    barrier = pltpu.get_barrier_semaphore()
    signal(barrier, (left, shell))
    pl.when(odd)(lambda: signal(barrier, (t, inner)))
    pl.when(odd & not_outermost)(lambda: signal(barrier, (t, outer)))
    pl.when(first_half)(lambda: signal(barrier, (opposite, shell)))

    place = lax.rem(t, PLANE)
    sender, receiver = place == PLANE - 1, place == 0
    relays = [place == relay for relay in RELAYS]
    relaying = functools.reduce(jnp.logical_or, relays)
    back_relay = place == BACK
    to_back = lax.rem(t + loop_size - PLANE + BACK, loop_size)
    back_from = lax.rem(t + PLANE - BACK, loop_size)
    last = lax.rem(t + PLANE - 1 - BACK, loop_size)
    known_back = lax.max(t - PLANE + 1 + BACK, 0)

    @pl.when(receiver)
    def _():
        for relay in RELAYS:
            signal(barrier, (lax.rem(t + relay, loop_size), shell))

    @pl.when(back_relay)
    def _():
        signal(barrier, (back_from, shell))
        signal(barrier, (last, shell))

    own = pltpu.make_async_copy(v, ext.at[:, pl.ds(2, width), pl.ds(PAD, rows), :], own_sem)

    even_inner, even_outer = even & not_innermost, even & not_outermost
    partners = 1 + even_inner.astype(jnp.int32) + even_outer.astype(jnp.int32) + second_half.astype(jnp.int32)
    partners += (relaying | receiver | sender).astype(jnp.int32)
    pl.semaphore_wait(barrier, partners)
    signal(ready.at[0], (right, shell))

    size = rows // PIECES
    tail = rows - len(RELAYS) * SHARE
    back_tail = rows - BACK_SHARE
    leftward_rows = [(back_tail, BACK_SHARE)] + [(p * size, min(size, back_tail - p * size)) for p in range(PIECES)]
    rightward_rows = [(tail + k * SHARE, SHARE) for k in range(len(RELAYS))]
    rightward_rows += [(p * size, min(size, tail - p * size)) for p in range(PIECES)]

    def layers_copy(d, p, start, count):
        at, src, dst = ((right, width - 2, 0), (left, 0, width + 2))[d]
        return pltpu.make_async_remote_copy(
            src_ref=v.at[:, pl.ds(src, 2), pl.ds(start, count), :],
            dst_ref=ext.at[:, pl.ds(dst, 2), pl.ds(PAD + start, count), :],
            send_sem=send_sem.at[d, p],
            recv_sem=recv_sem.at[d, p],
            device_id=(at, shell),
            device_id_type=MESH,
        )

    rightward = [layers_copy(0, p, *part) for p, part in enumerate(rightward_rows)]
    leftward = [layers_copy(1, p, *part) for p, part in enumerate(leftward_rows)]

    to_back_relay = pltpu.make_async_remote_copy(
        src_ref=v.at[:, pl.ds(0, 2), pl.ds(back_tail, BACK_SHARE), :],
        dst_ref=passing.at[:, :, pl.ds(0, BACK_SHARE), :],
        send_sem=send_sem.at[1, 0],
        recv_sem=relay_recv,
        device_id=(to_back, shell),
        device_id_type=MESH,
    )
    from_back_relay = pltpu.make_async_remote_copy(
        src_ref=passing.at[:, :, pl.ds(0, BACK_SHARE), :],
        dst_ref=ext.at[:, pl.ds(width + 2, 2), pl.ds(PAD + back_tail, BACK_SHARE), :],
        send_sem=relay_send,
        recv_sem=recv_sem.at[1, 0],
        device_id=(last, shell),
        device_id_type=MESH,
    )

    @pl.when(jnp.logical_not(sender))
    def _():
        for copy in rightward[: len(RELAYS)]:
            copy.start()

    takes_part = sender | relaying
    early_right, late_right = rightward[len(RELAYS) : len(RELAYS) + EARLY], rightward[len(RELAYS) + EARLY :]
    early_left, late_left = leftward[1:2], leftward[2:]
    for copy in early_right:
        copy.start()

    @pl.when(jnp.logical_not(takes_part))
    def _():
        for copy in late_right:
            copy.start()

    pl.when(sender)(lambda: signal(back_ready, (known_back, shell)))
    pl.when(even_inner)(lambda: signal(ready.at[1], (t, inner)))
    pl.when(even_outer)(lambda: signal(ready.at[3], (t, outer)))
    pl.when(second_half)(lambda: signal(ready.at[2], (opposite, shell)))
    for k, mine in enumerate(relays):
        pl.when(mine)(lambda: signal(passing_ready.at[k], (lax.max(t - RELAYS[k], 0), shell)))
    own.start()

    pl.when(receiver)(to_back_relay.start)

    first_plane = lax.rem(t, RUN) == 0

    def send_leftward():
        pl.semaphore_wait(ready.at[0], 1)
        pl.when(jnp.logical_not(receiver))(leftward[0].start)
        for copy in early_left:
            copy.start()

        @pl.when(jnp.logical_not(sender))
        def _():
            for copy in late_left:
                copy.start()

    pl.when(jnp.logical_not(first_plane))(send_leftward)

    own.wait()

    for c in range(3):
        for m in range(width):
            at = 2 * (c * width + m)
            head = ext[c, m + 2, PAD : PAD + 2, :]
            across = jnp.concatenate([head[1:2], head[0:1]], axis=0) * (1.0 if c == 2 else -1.0)
            stage[0, at : at + 2, :] = jnp.where(innermost, across, head)
            stage[1, at : at + 2, :] = ext[c, m + 2, top - 2 : top, :]

    def ghost_copy(src, dst, at):
        return pltpu.make_async_remote_copy(
            src_ref=stage.at[src],
            dst_ref=ghost.at[dst],
            send_sem=ghost_send.at[src],
            recv_sem=ghost_recv.at[dst],
            device_id=at,
            device_id_type=MESH,
        )

    across = ghost_copy(0, 0, (opposite, shell))
    inward = ghost_copy(0, 1, (t, inner))
    outward = ghost_copy(1, 0, (t, outer))
    pl.when(odd)(lambda: pl.semaphore_wait(ready.at[3], 1))
    pl.when(not_innermost)(inward.start)
    pl.when(odd & not_outermost)(lambda: pl.semaphore_wait(ready.at[1], 1))
    pl.when(not_outermost)(outward.start)

    pl.when(first_half)(lambda: pl.semaphore_wait(ready.at[2], 1))
    pl.when(innermost)(across.start)

    @pl.when(back_relay)
    def _():
        to_back_relay.wait_recv()
        pl.semaphore_wait(back_ready, 1)
        from_back_relay.start()

    pl.when(first_plane)(send_leftward)

    @pl.when(receiver)
    def _():
        for k in range(len(RELAYS)):
            pl.semaphore_wait(passing_ready.at[k], 1)
        signal(passing_ready.at[len(RELAYS)], (left, shell))


    blocks = rows // BLOCK

    @pl.loop(0, blocks)
    def _(b):
        row = pl.multiple_of(b * BLOCK, BLOCK)
        place = lax.broadcasted_iota(jnp.int32, (BLOCK, v.shape[3]), 0) + (shell * rows + row)
        place = place.astype(jnp.float32)
        weights[0, pl.ds(row, BLOCK), :] = 1.0 / (2.0 * place + 1.0)
        weights[1, pl.ds(row, BLOCK), :] = (place + 0.5) * (1.0 / grid_r)

    @pl.loop(0, blocks)
    def _(b):
        row = pl.multiple_of(b * BLOCK, BLOCK)
        for m in range(2, width - 2):
            azimuth_block(ext, weights, azimuth, m, row, grid_r, grid_t)

    def to_relay(k):
        return pltpu.make_async_remote_copy(
            src_ref=v.at[:, pl.ds(width - 2, 2), pl.ds(tail + k * SHARE, SHARE), :],
            dst_ref=passing.at[:, :, pl.ds(0, SHARE), :],
            send_sem=send_sem.at[0, k],
            recv_sem=relay_recv,
            device_id=(lax.rem(right + RELAYS[k], loop_size), shell),
            device_id_type=MESH,
        )

    def from_relay(k):
        return pltpu.make_async_remote_copy(
            src_ref=passing.at[:, :, pl.ds(0, SHARE), :],
            dst_ref=ext.at[:, pl.ds(0, 2), pl.ds(PAD + tail + k * SHARE, SHARE), :],
            send_sem=relay_send,
            recv_sem=recv_sem.at[0, k],
            device_id=(lax.max(t - RELAYS[k], 0), shell),
            device_id_type=MESH,
        )

    @pl.when(sender)
    def _():
        pl.semaphore_wait(passing_ready.at[len(RELAYS)], 1)
        for k in range(len(RELAYS)):
            to_relay(k).start()
        for copy in late_right + late_left:
            copy.start()

    half = rows // 2 - END

    @pl.loop(0, width)
    def _(m):
        radial_block(ext, weights, radial, m, END, half)
        radial_block(ext, weights, radial, m, END + half, half)

    for k, mine in enumerate(relays):

        @pl.when(mine)
        def _():
            to_relay(k).wait_recv()
            from_relay(k).start()

    @pl.when(relaying)
    def _():
        for copy in late_right:
            copy.start()

    across.wait_recv()
    pl.when(not_outermost)(inward.wait_recv)
    for c in range(3):
        for m in range(width):
            at = 2 * (c * width + m)
            ext[c, m + 2, PAD - 2 : PAD, :] = ghost[0, at : at + 2, :]
            last = ext[c, m + 2, top - 2 : top, :]
            wall = jnp.concatenate([last[1:2], last[0:1]], axis=0) * -1.0
            ext[c, m + 2, top : top + 2, :] = jnp.where(outermost, wall, ghost[1, at : at + 2, :])

    @pl.loop(0, width // 2)
    def _(k):
        for m in (2 * k, 2 * k + 1):
            radial_block(ext, weights, radial, m, 0, END)
            radial_block(ext, weights, radial, m, rows - END, END)

    def edge_rows(m, start, count):
        @pl.loop(start // BLOCK, (start + count) // BLOCK)
        def _(b):
            row = pl.multiple_of(b * BLOCK, BLOCK)
            azimuth_block(ext, weights, azimuth, m, row, grid_r, grid_t)
            azimuth_block(ext, weights, azimuth, m + 1, row, grid_r, grid_t)

    leftward[0].wait_recv()
    for copy, part in zip(leftward[1:], leftward_rows[1:]):
        copy.wait_recv()
        edge_rows(width - 2, part[0], size)

    for copy in rightward[: len(RELAYS)]:
        copy.wait_recv()
    for copy, part in zip(rightward[len(RELAYS) :], rightward_rows[len(RELAYS) :]):
        copy.wait_recv()
        edge_rows(0, part[0], size)

    for k, mine in enumerate(relays):
        pl.when(mine)(from_relay(k).wait_send)
    pl.when(back_relay)(from_back_relay.wait_send)
    for copy in rightward + leftward:
        copy.wait_send()
    inward.wait_send()
    pl.when(not_outermost)(outward.wait_send)


def write_out(radial_in, azimuth_in, radial, azimuth, sems):
    copies = []
    for k, (src, dst) in enumerate(((radial_in, radial), (azimuth_in, azimuth))):
        for c in range(3):
            copies.append(pltpu.make_async_copy(src.at[c], dst.at[c], sems.at[k, c]))
    for copy in copies:
        copy.start()
    for copy in copies:
        copy.wait()


def solution(mesh):
    loop_size, shells = mesh.shape["theta"], mesh.shape["row"]

    def per_device(v):
        _, width, rows, planes = v.shape
        result = jax.ShapeDtypeStruct(v.shape, jnp.bfloat16)
        held = pltpu.VMEM(v.shape, jnp.bfloat16)
        vmem = pl.BlockSpec(memory_space=pltpu.VMEM)
        hbm = pl.BlockSpec(memory_space=pltpu.HBM)
        dma = pltpu.SemaphoreType.DMA
        radial, azimuth = pl.pallas_call(
            functools.partial(tendencies, loop_size, shells),
            out_shape=(held, held),
            in_specs=[hbm],
            out_specs=(vmem, vmem),
            scratch_shapes=[
                pltpu.VMEM((3, width + 4, rows + 2 * PAD, planes), jnp.float32),
                pltpu.VMEM((2, rows, planes), jnp.float32),
                pltpu.VMEM((2, 6 * width, planes), jnp.float32),
                pltpu.VMEM((2, 6 * width, planes), jnp.float32),
                dma,
                dma((2, PIECES + 1)),
                dma((2, PIECES + 1)),
                dma((2,)),
                dma((2,)),
                pltpu.SemaphoreType.REGULAR((4,)),
                pltpu.VMEM((3, 2, max(SHARE, BACK_SHARE), planes), jnp.float32),
                pltpu.SemaphoreType.REGULAR((len(RELAYS) + 1,)),
                pltpu.SemaphoreType.REGULAR,
                dma,
                dma,
            ],
            compiler_params=pltpu.CompilerParams(
                collective_id=0, has_side_effects=True, vmem_limit_bytes=32 << 20
            ),
        )(pltpu.with_memory_space_constraint(v, pltpu.HBM))
        radial = pltpu.with_memory_space_constraint(radial, pltpu.VMEM)
        azimuth = pltpu.with_memory_space_constraint(azimuth, pltpu.VMEM)
        return pl.pallas_call(
            write_out,
            out_shape=(result, result),
            in_specs=[vmem, vmem],
            out_specs=(hbm, hbm),
            scratch_shapes=[dma((2, 3))],
            compiler_params=pltpu.CompilerParams(vmem_limit_bytes=32 << 20),
        )(radial, azimuth)

    spec = P(None, "theta", "row", None)
    return jax.shard_map(
        per_device, mesh=mesh, in_specs=(spec,), out_specs=(spec, spec), check_vma=False
    )
```

```python
import functools
import math

import jax
import jax.numpy as jnp
from jax import lax
from jax.experimental import pallas as pl
from jax.experimental.pallas import tpu as pltpu
from jax.sharding import PartitionSpec as P

MESH = pl.DeviceIdType.MESH
PAD = 8
BLOCK = 32
RUN = 8
PLANE = 32
RELAYS = (7,)
BACK = 24
SHARE = 24
BACK_SHARE = 24
EARLY = 3
END = 16
PIECES = 4


def radial_block(ext, weights, out, m, row, count):
    slope_r = 0.2 / 12.0
    slope_z = 0.2 / 48.0
    lap_r = 0.1
    lap_z = 0.1 / 16.0
    mid = pl.ds(row + PAD, count)
    inverse = weights[0, pl.ds(row, count), :]
    u_rad = ext[0, m + 2, mid, :]
    u_ax = ext[2, m + 2, mid, :]
    radial_two = u_rad * (-slope_r)
    radial_one = radial_two * 8.0 + lap_r * inverse
    axial_two = u_ax * (-slope_z)
    axial_one = axial_two * 8.0
    for c in range(3):
        f = ext[c, m + 2, mid, :]
        out_one = ext[c, m + 2, pl.ds(row + PAD + 1, count), :]
        in_one = ext[c, m + 2, pl.ds(row + PAD - 1, count), :]
        out_two = ext[c, m + 2, pl.ds(row + PAD + 2, count), :]
        in_two = ext[c, m + 2, pl.ds(row + PAD - 2, count), :]
        planes = f.shape[1]
        ahead_one = pltpu.roll(f, planes - 1, 1)
        behind_one = pltpu.roll(f, 1, 1)
        ahead_two = pltpu.roll(f, planes - 2, 1)
        behind_two = pltpu.roll(f, 2, 1)
        total = (out_one - in_one) * radial_one - (out_two - in_two) * radial_two
        total += (ahead_one - behind_one) * axial_one - (ahead_two - behind_two) * axial_two
        total += (out_one + in_one) * lap_r + (ahead_one + behind_one) * lap_z
        total -= f * (2.0 * (lap_r + lap_z))
        out[c, m, pl.ds(row, count), :] = total.astype(out.dtype)


def azimuth_block(ext, weights, out, m, row, grid_r, grid_t):
    step = 2.0 * math.pi / grid_t
    angle_time = 2.0 / grid_r
    small = angle_time * 0.5 / grid_r
    lap = small / (step * step)
    slope = 8.0 / (12.0 * step)
    mid = pl.ds(row + PAD, BLOCK)
    radius = weights[1, pl.ds(row, BLOCK), :] * angle_time
    u_rad = ext[0, m + 2, mid, :]
    u_ang = ext[1, m + 2, mid, :]
    carried = radius * u_ang
    slopes, totals = [], []
    for c in range(3):
        f = u_rad if c == 0 else u_ang if c == 1 else ext[c, m + 2, mid, :]
        up = ext[c, m + 3, mid, :]
        down = ext[c, m + 1, mid, :]
        wide = ext[c, m + 4, mid, :] - ext[c, m, mid, :]
        slopes.append(((up - down) - wide * 0.125) * slope)
        totals.append((up + down) * lap - f * (2.0 * lap if c == 2 else 2.0 * lap + small))
    totals[0] += carried * (u_ang - slopes[0]) - slopes[1] * (2.0 * small)
    totals[1] += slopes[0] * (2.0 * small) - carried * (u_rad + slopes[1])
    totals[2] -= carried * slopes[2]
    for c in range(3):
        out[c, m, pl.ds(row, BLOCK), :] = totals[c].astype(out.dtype)


def tendencies(
    loop_size, shells, v, radial, azimuth, ext, weights, stage, ghost,
    own_sem, send_sem, recv_sem, ghost_send, ghost_recv, ready, passing, passing_ready, back_ready, relay_send, relay_recv,
):
    width, rows = v.shape[1], v.shape[2]
    grid_r, grid_t = rows * shells, width * loop_size
    top = rows + PAD
    t = lax.axis_index("theta")
    shell = lax.axis_index("row")
    right, left = lax.rem(t + 1, loop_size), lax.rem(t + loop_size - 1, loop_size)
    opposite = lax.rem(t + loop_size // 2, loop_size)
    innermost, outermost = shell == 0, shell == shells - 1
    not_innermost, not_outermost = shell > 0, shell < shells - 1
    first_half = innermost & (t < loop_size // 2)
    second_half = innermost & (t >= loop_size // 2)
    inner = lax.max(shell - 1, 0)
    outer = lax.min(shell + 1, shells - 1)

    def signal(sem, at):
        pl.semaphore_signal(sem, inc=1, device_id=at, device_id_type=MESH)

    odd = lax.rem(shell, 2) == 1
    even = jnp.logical_not(odd)
    barrier = pltpu.get_barrier_semaphore()
    signal(barrier, (left, shell))
    pl.when(odd)(lambda: signal(barrier, (t, inner)))
    pl.when(odd & not_outermost)(lambda: signal(barrier, (t, outer)))
    pl.when(first_half)(lambda: signal(barrier, (opposite, shell)))

    place = lax.rem(t, PLANE)
    sender, receiver = place == PLANE - 1, place == 0
    relays = [place == relay for relay in RELAYS]
    relaying = functools.reduce(jnp.logical_or, relays)
    back_relay = place == BACK
    to_back = lax.rem(t + loop_size - PLANE + BACK, loop_size)
    back_from = lax.rem(t + PLANE - BACK, loop_size)
    last = lax.rem(t + PLANE - 1 - BACK, loop_size)
    known_back = lax.max(t - PLANE + 1 + BACK, 0)

    @pl.when(receiver)
    def _():
        for relay in RELAYS:
            signal(barrier, (lax.rem(t + relay, loop_size), shell))

    @pl.when(back_relay)
    def _():
        signal(barrier, (back_from, shell))
        signal(barrier, (last, shell))

    own = pltpu.make_async_copy(v, ext.at[:, pl.ds(2, width), pl.ds(PAD, rows), :], own_sem)

    even_inner, even_outer = even & not_innermost, even & not_outermost
    partners = 1 + even_inner.astype(jnp.int32) + even_outer.astype(jnp.int32) + second_half.astype(jnp.int32)
    partners += (relaying | receiver | sender).astype(jnp.int32)
    pl.semaphore_wait(barrier, partners)
    signal(ready.at[0], (right, shell))

    size = rows // PIECES
    tail = rows - len(RELAYS) * SHARE
    back_tail = rows - BACK_SHARE
    leftward_rows = [(back_tail, BACK_SHARE)] + [(p * size, min(size, back_tail - p * size)) for p in range(PIECES)]
    rightward_rows = [(tail + k * SHARE, SHARE) for k in range(len(RELAYS))]
    rightward_rows += [(p * size, min(size, tail - p * size)) for p in range(PIECES)]

    def layers_copy(d, p, start, count):
        at, src, dst = ((right, width - 2, 0), (left, 0, width + 2))[d]
        return pltpu.make_async_remote_copy(
            src_ref=v.at[:, pl.ds(src, 2), pl.ds(start, count), :],
            dst_ref=ext.at[:, pl.ds(dst, 2), pl.ds(PAD + start, count), :],
            send_sem=send_sem.at[d, p],
            recv_sem=recv_sem.at[d, p],
            device_id=(at, shell),
            device_id_type=MESH,
        )

    rightward = [layers_copy(0, p, *part) for p, part in enumerate(rightward_rows)]
    leftward = [layers_copy(1, p, *part) for p, part in enumerate(leftward_rows)]

    to_back_relay = pltpu.make_async_remote_copy(
        src_ref=v.at[:, pl.ds(0, 2), pl.ds(back_tail, BACK_SHARE), :],
        dst_ref=passing.at[:, :, pl.ds(0, BACK_SHARE), :],
        send_sem=send_sem.at[1, 0],
        recv_sem=relay_recv,
        device_id=(to_back, shell),
        device_id_type=MESH,
    )
    from_back_relay = pltpu.make_async_remote_copy(
        src_ref=passing.at[:, :, pl.ds(0, BACK_SHARE), :],
        dst_ref=ext.at[:, pl.ds(width + 2, 2), pl.ds(PAD + back_tail, BACK_SHARE), :],
        send_sem=relay_send,
        recv_sem=recv_sem.at[1, 0],
        device_id=(last, shell),
        device_id_type=MESH,
    )

    @pl.when(jnp.logical_not(sender))
    def _():
        for copy in rightward[: len(RELAYS)]:
            copy.start()

    takes_part = sender | relaying
    early_right, late_right = rightward[len(RELAYS) : len(RELAYS) + EARLY], rightward[len(RELAYS) + EARLY :]
    early_left, late_left = leftward[1:2], leftward[2:]
    for copy in early_right:
        copy.start()

    @pl.when(jnp.logical_not(takes_part))
    def _():
        for copy in late_right:
            copy.start()

    pl.when(sender)(lambda: signal(back_ready, (known_back, shell)))
    pl.when(even_inner)(lambda: signal(ready.at[1], (t, inner)))
    pl.when(even_outer)(lambda: signal(ready.at[3], (t, outer)))
    pl.when(second_half)(lambda: signal(ready.at[2], (opposite, shell)))
    for k, mine in enumerate(relays):
        pl.when(mine)(lambda: signal(passing_ready.at[k], (lax.max(t - RELAYS[k], 0), shell)))
    own.start()

    pl.when(receiver)(to_back_relay.start)

    first_plane = lax.rem(t, RUN) == 0

    def send_leftward():
        pl.semaphore_wait(ready.at[0], 1)
        pl.when(jnp.logical_not(receiver))(leftward[0].start)
        for copy in early_left:
            copy.start()

        @pl.when(jnp.logical_not(sender))
        def _():
            for copy in late_left:
                copy.start()

    pl.when(jnp.logical_not(first_plane))(send_leftward)

    own.wait()

    for c in range(3):
        for m in range(width):
            at = 2 * (c * width + m)
            head = ext[c, m + 2, PAD : PAD + 2, :]
            across = jnp.concatenate([head[1:2], head[0:1]], axis=0) * (1.0 if c == 2 else -1.0)
            stage[0, at : at + 2, :] = jnp.where(innermost, across, head)
            stage[1, at : at + 2, :] = ext[c, m + 2, top - 2 : top, :]

    def ghost_copy(src, dst, at):
        return pltpu.make_async_remote_copy(
            src_ref=stage.at[src],
            dst_ref=ghost.at[dst],
            send_sem=ghost_send.at[src],
            recv_sem=ghost_recv.at[dst],
            device_id=at,
            device_id_type=MESH,
        )

    across = ghost_copy(0, 0, (opposite, shell))
    inward = ghost_copy(0, 1, (t, inner))
    outward = ghost_copy(1, 0, (t, outer))
    pl.when(odd)(lambda: pl.semaphore_wait(ready.at[3], 1))
    pl.when(not_innermost)(inward.start)
    pl.when(odd & not_outermost)(lambda: pl.semaphore_wait(ready.at[1], 1))
    pl.when(not_outermost)(outward.start)

    pl.when(first_half)(lambda: pl.semaphore_wait(ready.at[2], 1))
    pl.when(innermost)(across.start)

    @pl.when(back_relay)
    def _():
        to_back_relay.wait_recv()
        pl.semaphore_wait(back_ready, 1)
        from_back_relay.start()

    pl.when(first_plane)(send_leftward)

    @pl.when(receiver)
    def _():
        for k in range(len(RELAYS)):
            pl.semaphore_wait(passing_ready.at[k], 1)
        signal(passing_ready.at[len(RELAYS)], (left, shell))


    blocks = rows // BLOCK

    @pl.loop(0, blocks)
    def _(b):
        row = pl.multiple_of(b * BLOCK, BLOCK)
        place = lax.broadcasted_iota(jnp.int32, (BLOCK, v.shape[3]), 0) + (shell * rows + row)
        place = place.astype(jnp.float32)
        weights[0, pl.ds(row, BLOCK), :] = 1.0 / (2.0 * place + 1.0)
        weights[1, pl.ds(row, BLOCK), :] = (place + 0.5) * (1.0 / grid_r)

    @pl.loop(0, blocks)
    def _(b):
        row = pl.multiple_of(b * BLOCK, BLOCK)
        for m in range(2, width - 2):
            azimuth_block(ext, weights, azimuth, m, row, grid_r, grid_t)

    def to_relay(k):
        return pltpu.make_async_remote_copy(
            src_ref=v.at[:, pl.ds(width - 2, 2), pl.ds(tail + k * SHARE, SHARE), :],
            dst_ref=passing.at[:, :, pl.ds(0, SHARE), :],
            send_sem=send_sem.at[0, k],
            recv_sem=relay_recv,
            device_id=(lax.rem(right + RELAYS[k], loop_size), shell),
            device_id_type=MESH,
        )

    def from_relay(k):
        return pltpu.make_async_remote_copy(
            src_ref=passing.at[:, :, pl.ds(0, SHARE), :],
            dst_ref=ext.at[:, pl.ds(0, 2), pl.ds(PAD + tail + k * SHARE, SHARE), :],
            send_sem=relay_send,
            recv_sem=recv_sem.at[0, k],
            device_id=(lax.max(t - RELAYS[k], 0), shell),
            device_id_type=MESH,
        )

    @pl.when(sender)
    def _():
        pl.semaphore_wait(passing_ready.at[len(RELAYS)], 1)
        for k in range(len(RELAYS)):
            to_relay(k).start()
        for copy in late_right + late_left:
            copy.start()

    half = rows // 2 - END

    @pl.loop(0, width)
    def _(m):
        radial_block(ext, weights, radial, m, END, half)
        radial_block(ext, weights, radial, m, END + half, half)

    for k, mine in enumerate(relays):

        @pl.when(mine)
        def _():
            to_relay(k).wait_recv()
            from_relay(k).start()

    @pl.when(relaying)
    def _():
        for copy in late_right:
            copy.start()

    across.wait_recv()
    pl.when(not_outermost)(inward.wait_recv)
    for c in range(3):
        for m in range(width):
            at = 2 * (c * width + m)
            ext[c, m + 2, PAD - 2 : PAD, :] = ghost[0, at : at + 2, :]
            last = ext[c, m + 2, top - 2 : top, :]
            wall = jnp.concatenate([last[1:2], last[0:1]], axis=0) * -1.0
            ext[c, m + 2, top : top + 2, :] = jnp.where(outermost, wall, ghost[1, at : at + 2, :])

    @pl.loop(0, width // 2)
    def _(k):
        for m in (2 * k, 2 * k + 1):
            radial_block(ext, weights, radial, m, 0, END)
            radial_block(ext, weights, radial, m, rows - END, END)

    def edge_rows(m, start, count):
        @pl.loop(start // BLOCK, (start + count) // BLOCK)
        def _(b):
            row = pl.multiple_of(b * BLOCK, BLOCK)
            azimuth_block(ext, weights, azimuth, m, row, grid_r, grid_t)
            azimuth_block(ext, weights, azimuth, m + 1, row, grid_r, grid_t)

    leftward[0].wait_recv()
    for copy, part in zip(leftward[1:], leftward_rows[1:]):
        copy.wait_recv()
        edge_rows(width - 2, part[0], size)

    for copy in rightward[: len(RELAYS)]:
        copy.wait_recv()
    for copy, part in zip(rightward[len(RELAYS) :], rightward_rows[len(RELAYS) :]):
        copy.wait_recv()
        edge_rows(0, part[0], size)

    for k, mine in enumerate(relays):
        pl.when(mine)(from_relay(k).wait_send)
    pl.when(back_relay)(from_back_relay.wait_send)
    for copy in rightward + leftward:
        copy.wait_send()
    inward.wait_send()
    pl.when(not_outermost)(outward.wait_send)


def write_out(radial_in, azimuth_in, radial, azimuth, sems):
    copies = []
    for k, (src, dst) in enumerate(((radial_in, radial), (azimuth_in, azimuth))):
        for c in range(3):
            copies.append(pltpu.make_async_copy(src.at[c], dst.at[c], sems.at[k, c]))
    for copy in copies:
        copy.start()
    for copy in copies:
        copy.wait()


def solution(mesh):
    loop_size, shells = mesh.shape["theta"], mesh.shape["row"]

    def per_device(v):
        _, width, rows, planes = v.shape
        result = jax.ShapeDtypeStruct(v.shape, jnp.bfloat16)
        held = pltpu.VMEM(v.shape, jnp.bfloat16)
        vmem = pl.BlockSpec(memory_space=pltpu.VMEM)
        hbm = pl.BlockSpec(memory_space=pltpu.HBM)
        dma = pltpu.SemaphoreType.DMA
        radial, azimuth = pl.pallas_call(
            functools.partial(tendencies, loop_size, shells),
            out_shape=(held, held),
            in_specs=[hbm],
            out_specs=(vmem, vmem),
            scratch_shapes=[
                pltpu.VMEM((3, width + 4, rows + 2 * PAD, planes), jnp.float32),
                pltpu.VMEM((2, rows, planes), jnp.float32),
                pltpu.VMEM((2, 6 * width, planes), jnp.float32),
                pltpu.VMEM((2, 6 * width, planes), jnp.float32),
                dma,
                dma((2, PIECES + 1)),
                dma((2, PIECES + 1)),
                dma((2,)),
                dma((2,)),
                pltpu.SemaphoreType.REGULAR((4,)),
                pltpu.VMEM((3, 2, max(SHARE, BACK_SHARE), planes), jnp.float32),
                pltpu.SemaphoreType.REGULAR((len(RELAYS) + 1,)),
                pltpu.SemaphoreType.REGULAR,
                dma,
                dma,
            ],
            compiler_params=pltpu.CompilerParams(
                collective_id=0, has_side_effects=True, vmem_limit_bytes=32 << 20
            ),
        )(pltpu.with_memory_space_constraint(v, pltpu.HBM))
        radial = pltpu.with_memory_space_constraint(radial, pltpu.VMEM)
        azimuth = pltpu.with_memory_space_constraint(azimuth, pltpu.VMEM)
        return pl.pallas_call(
            write_out,
            out_shape=(result, result),
            in_specs=[vmem, vmem],
            out_specs=(hbm, hbm),
            scratch_shapes=[dma((2, 3))],
            compiler_params=pltpu.CompilerParams(vmem_limit_bytes=32 << 20),
        )(radial, azimuth)

    spec = P(None, "theta", "row", None)
    return jax.shard_map(
        per_device, mesh=mesh, in_specs=(spec,), out_specs=(spec, spec), check_vma=False
    )
```

```python
import functools
import math

import jax
import jax.numpy as jnp
from jax import lax
from jax.experimental import pallas as pl
from jax.experimental.pallas import tpu as pltpu
from jax.sharding import PartitionSpec as P

MESH = pl.DeviceIdType.MESH
PAD = 8
BLOCK = 32
RUN = 8
PLANE = 32
RELAYS = (7,)
BACK = 24
SHARE = 24
BACK_SHARE = 24
EARLY = 2
END = 16
PIECES = 4


def radial_block(ext, weights, out, m, row, count):
    slope_r = 0.2 / 12.0
    slope_z = 0.2 / 48.0
    lap_r = 0.1
    lap_z = 0.1 / 16.0
    mid = pl.ds(row + PAD, count)
    inverse = weights[0, pl.ds(row, count), :]
    u_rad = ext[0, m + 2, mid, :]
    u_ax = ext[2, m + 2, mid, :]
    radial_two = u_rad * (-slope_r)
    radial_one = radial_two * 8.0 + lap_r * inverse
    axial_two = u_ax * (-slope_z)
    axial_one = axial_two * 8.0
    for c in range(3):
        f = ext[c, m + 2, mid, :]
        out_one = ext[c, m + 2, pl.ds(row + PAD + 1, count), :]
        in_one = ext[c, m + 2, pl.ds(row + PAD - 1, count), :]
        out_two = ext[c, m + 2, pl.ds(row + PAD + 2, count), :]
        in_two = ext[c, m + 2, pl.ds(row + PAD - 2, count), :]
        planes = f.shape[1]
        ahead_one = pltpu.roll(f, planes - 1, 1)
        behind_one = pltpu.roll(f, 1, 1)
        ahead_two = pltpu.roll(f, planes - 2, 1)
        behind_two = pltpu.roll(f, 2, 1)
        total = (out_one - in_one) * radial_one - (out_two - in_two) * radial_two
        total += (ahead_one - behind_one) * axial_one - (ahead_two - behind_two) * axial_two
        total += (out_one + in_one) * lap_r + (ahead_one + behind_one) * lap_z
        total -= f * (2.0 * (lap_r + lap_z))
        out[c, m, pl.ds(row, count), :] = total.astype(out.dtype)


def azimuth_block(ext, weights, out, m, row, grid_r, grid_t):
    step = 2.0 * math.pi / grid_t
    angle_time = 2.0 / grid_r
    small = angle_time * 0.5 / grid_r
    lap = small / (step * step)
    slope = 8.0 / (12.0 * step)
    mid = pl.ds(row + PAD, BLOCK)
    radius = weights[1, pl.ds(row, BLOCK), :] * angle_time
    u_rad = ext[0, m + 2, mid, :]
    u_ang = ext[1, m + 2, mid, :]
    carried = radius * u_ang
    slopes, totals = [], []
    for c in range(3):
        f = u_rad if c == 0 else u_ang if c == 1 else ext[c, m + 2, mid, :]
        up = ext[c, m + 3, mid, :]
        down = ext[c, m + 1, mid, :]
        wide = ext[c, m + 4, mid, :] - ext[c, m, mid, :]
        slopes.append(((up - down) - wide * 0.125) * slope)
        totals.append((up + down) * lap - f * (2.0 * lap if c == 2 else 2.0 * lap + small))
    totals[0] += carried * (u_ang - slopes[0]) - slopes[1] * (2.0 * small)
    totals[1] += slopes[0] * (2.0 * small) - carried * (u_rad + slopes[1])
    totals[2] -= carried * slopes[2]
    for c in range(3):
        out[c, m, pl.ds(row, BLOCK), :] = totals[c].astype(out.dtype)


def tendencies(
    loop_size, shells, v, radial, azimuth, ext, weights, stage, ghost,
    own_sem, send_sem, recv_sem, ghost_send, ghost_recv, ready, passing, passing_ready, back_ready, relay_send, relay_recv,
):
    width, rows = v.shape[1], v.shape[2]
    grid_r, grid_t = rows * shells, width * loop_size
    top = rows + PAD
    t = lax.axis_index("theta")
    shell = lax.axis_index("row")
    right, left = lax.rem(t + 1, loop_size), lax.rem(t + loop_size - 1, loop_size)
    opposite = lax.rem(t + loop_size // 2, loop_size)
    innermost, outermost = shell == 0, shell == shells - 1
    not_innermost, not_outermost = shell > 0, shell < shells - 1
    first_half = innermost & (t < loop_size // 2)
    second_half = innermost & (t >= loop_size // 2)
    inner = lax.max(shell - 1, 0)
    outer = lax.min(shell + 1, shells - 1)

    def signal(sem, at):
        pl.semaphore_signal(sem, inc=1, device_id=at, device_id_type=MESH)

    odd = lax.rem(shell, 2) == 1
    even = jnp.logical_not(odd)
    barrier = pltpu.get_barrier_semaphore()
    signal(barrier, (left, shell))
    pl.when(odd)(lambda: signal(barrier, (t, inner)))
    pl.when(odd & not_outermost)(lambda: signal(barrier, (t, outer)))
    pl.when(first_half)(lambda: signal(barrier, (opposite, shell)))

    place = lax.rem(t, PLANE)
    sender, receiver = place == PLANE - 1, place == 0
    relays = [place == relay for relay in RELAYS]
    relaying = functools.reduce(jnp.logical_or, relays)
    back_relay = place == BACK
    to_back = lax.rem(t + loop_size - PLANE + BACK, loop_size)
    back_from = lax.rem(t + PLANE - BACK, loop_size)
    last = lax.rem(t + PLANE - 1 - BACK, loop_size)
    known_back = lax.max(t - PLANE + 1 + BACK, 0)

    @pl.when(receiver)
    def _():
        for relay in RELAYS:
            signal(barrier, (lax.rem(t + relay, loop_size), shell))

    @pl.when(back_relay)
    def _():
        signal(barrier, (back_from, shell))
        signal(barrier, (last, shell))

    own = pltpu.make_async_copy(v, ext.at[:, pl.ds(2, width), pl.ds(PAD, rows), :], own_sem)

    even_inner, even_outer = even & not_innermost, even & not_outermost
    partners = 1 + even_inner.astype(jnp.int32) + even_outer.astype(jnp.int32) + second_half.astype(jnp.int32)
    partners += (relaying | receiver | sender).astype(jnp.int32)
    pl.semaphore_wait(barrier, partners)
    signal(ready.at[0], (right, shell))

    size = rows // PIECES
    tail = rows - len(RELAYS) * SHARE
    back_tail = rows - BACK_SHARE
    leftward_rows = [(back_tail, BACK_SHARE)] + [(p * size, min(size, back_tail - p * size)) for p in range(PIECES)]
    rightward_rows = [(tail + k * SHARE, SHARE) for k in range(len(RELAYS))]
    rightward_rows += [(p * size, min(size, tail - p * size)) for p in range(PIECES)]

    def layers_copy(d, p, start, count):
        at, src, dst = ((right, width - 2, 0), (left, 0, width + 2))[d]
        return pltpu.make_async_remote_copy(
            src_ref=v.at[:, pl.ds(src, 2), pl.ds(start, count), :],
            dst_ref=ext.at[:, pl.ds(dst, 2), pl.ds(PAD + start, count), :],
            send_sem=send_sem.at[d, p],
            recv_sem=recv_sem.at[d, p],
            device_id=(at, shell),
            device_id_type=MESH,
        )

    rightward = [layers_copy(0, p, *part) for p, part in enumerate(rightward_rows)]
    leftward = [layers_copy(1, p, *part) for p, part in enumerate(leftward_rows)]

    to_back_relay = pltpu.make_async_remote_copy(
        src_ref=v.at[:, pl.ds(0, 2), pl.ds(back_tail, BACK_SHARE), :],
        dst_ref=passing.at[:, :, pl.ds(0, BACK_SHARE), :],
        send_sem=send_sem.at[1, 0],
        recv_sem=relay_recv,
        device_id=(to_back, shell),
        device_id_type=MESH,
    )
    from_back_relay = pltpu.make_async_remote_copy(
        src_ref=passing.at[:, :, pl.ds(0, BACK_SHARE), :],
        dst_ref=ext.at[:, pl.ds(width + 2, 2), pl.ds(PAD + back_tail, BACK_SHARE), :],
        send_sem=relay_send,
        recv_sem=recv_sem.at[1, 0],
        device_id=(last, shell),
        device_id_type=MESH,
    )

    @pl.when(jnp.logical_not(sender))
    def _():
        for copy in rightward[: len(RELAYS)]:
            copy.start()

    takes_part = sender | relaying
    early_right, late_right = rightward[len(RELAYS) : len(RELAYS) + EARLY], rightward[len(RELAYS) + EARLY :]
    early_left, late_left = leftward[1:2], leftward[2:]
    for copy in early_right:
        copy.start()

    @pl.when(jnp.logical_not(takes_part))
    def _():
        for copy in late_right:
            copy.start()

    pl.when(sender)(lambda: signal(back_ready, (known_back, shell)))
    pl.when(even_inner)(lambda: signal(ready.at[1], (t, inner)))
    pl.when(even_outer)(lambda: signal(ready.at[3], (t, outer)))
    pl.when(second_half)(lambda: signal(ready.at[2], (opposite, shell)))
    for k, mine in enumerate(relays):
        pl.when(mine)(lambda: signal(passing_ready.at[k], (lax.max(t - RELAYS[k], 0), shell)))
    own.start()

    pl.when(receiver)(to_back_relay.start)

    first_plane = lax.rem(t, RUN) == 0

    def send_leftward():
        pl.semaphore_wait(ready.at[0], 1)
        pl.when(jnp.logical_not(receiver))(leftward[0].start)
        for copy in early_left:
            copy.start()

        @pl.when(jnp.logical_not(sender))
        def _():
            for copy in late_left:
                copy.start()

    pl.when(jnp.logical_not(first_plane))(send_leftward)

    own.wait()

    for c in range(3):
        for m in range(width):
            at = 2 * (c * width + m)
            head = ext[c, m + 2, PAD : PAD + 2, :]
            across = jnp.concatenate([head[1:2], head[0:1]], axis=0) * (1.0 if c == 2 else -1.0)
            stage[0, at : at + 2, :] = jnp.where(innermost, across, head)
            stage[1, at : at + 2, :] = ext[c, m + 2, top - 2 : top, :]

    def ghost_copy(src, dst, at):
        return pltpu.make_async_remote_copy(
            src_ref=stage.at[src],
            dst_ref=ghost.at[dst],
            send_sem=ghost_send.at[src],
            recv_sem=ghost_recv.at[dst],
            device_id=at,
            device_id_type=MESH,
        )

    across = ghost_copy(0, 0, (opposite, shell))
    inward = ghost_copy(0, 1, (t, inner))
    outward = ghost_copy(1, 0, (t, outer))
    pl.when(odd)(lambda: pl.semaphore_wait(ready.at[3], 1))
    pl.when(not_innermost)(inward.start)
    pl.when(odd & not_outermost)(lambda: pl.semaphore_wait(ready.at[1], 1))
    pl.when(not_outermost)(outward.start)

    pl.when(first_half)(lambda: pl.semaphore_wait(ready.at[2], 1))
    pl.when(innermost)(across.start)

    @pl.when(back_relay)
    def _():
        to_back_relay.wait_recv()
        pl.semaphore_wait(back_ready, 1)
        from_back_relay.start()

    pl.when(first_plane)(send_leftward)

    @pl.when(receiver)
    def _():
        for k in range(len(RELAYS)):
            pl.semaphore_wait(passing_ready.at[k], 1)
        signal(passing_ready.at[len(RELAYS)], (left, shell))


    blocks = rows // BLOCK

    @pl.loop(0, blocks)
    def _(b):
        row = pl.multiple_of(b * BLOCK, BLOCK)
        place = lax.broadcasted_iota(jnp.int32, (BLOCK, v.shape[3]), 0) + (shell * rows + row)
        place = place.astype(jnp.float32)
        weights[0, pl.ds(row, BLOCK), :] = 1.0 / (2.0 * place + 1.0)
        weights[1, pl.ds(row, BLOCK), :] = (place + 0.5) * (1.0 / grid_r)

    @pl.loop(0, blocks)
    def _(b):
        row = pl.multiple_of(b * BLOCK, BLOCK)
        for m in range(2, width - 2):
            azimuth_block(ext, weights, azimuth, m, row, grid_r, grid_t)

    def to_relay(k):
        return pltpu.make_async_remote_copy(
            src_ref=v.at[:, pl.ds(width - 2, 2), pl.ds(tail + k * SHARE, SHARE), :],
            dst_ref=passing.at[:, :, pl.ds(0, SHARE), :],
            send_sem=send_sem.at[0, k],
            recv_sem=relay_recv,
            device_id=(lax.rem(right + RELAYS[k], loop_size), shell),
            device_id_type=MESH,
        )

    def from_relay(k):
        return pltpu.make_async_remote_copy(
            src_ref=passing.at[:, :, pl.ds(0, SHARE), :],
            dst_ref=ext.at[:, pl.ds(0, 2), pl.ds(PAD + tail + k * SHARE, SHARE), :],
            send_sem=relay_send,
            recv_sem=recv_sem.at[0, k],
            device_id=(lax.max(t - RELAYS[k], 0), shell),
            device_id_type=MESH,
        )

    @pl.when(sender)
    def _():
        pl.semaphore_wait(passing_ready.at[len(RELAYS)], 1)
        for k in range(len(RELAYS)):
            to_relay(k).start()
        for copy in late_right + late_left:
            copy.start()

    half = rows // 2 - END

    @pl.loop(0, width)
    def _(m):
        radial_block(ext, weights, radial, m, END, half)
        radial_block(ext, weights, radial, m, END + half, half)

    for k, mine in enumerate(relays):

        @pl.when(mine)
        def _():
            to_relay(k).wait_recv()
            from_relay(k).start()

    @pl.when(relaying)
    def _():
        for copy in late_right:
            copy.start()

    across.wait_recv()
    pl.when(not_outermost)(inward.wait_recv)
    for c in range(3):
        for m in range(width):
            at = 2 * (c * width + m)
            ext[c, m + 2, PAD - 2 : PAD, :] = ghost[0, at : at + 2, :]
            last = ext[c, m + 2, top - 2 : top, :]
            wall = jnp.concatenate([last[1:2], last[0:1]], axis=0) * -1.0
            ext[c, m + 2, top : top + 2, :] = jnp.where(outermost, wall, ghost[1, at : at + 2, :])

    @pl.loop(0, width // 2)
    def _(k):
        for m in (2 * k, 2 * k + 1):
            radial_block(ext, weights, radial, m, 0, END)
            radial_block(ext, weights, radial, m, rows - END, END)

    def edge_rows(m, start, count):
        @pl.loop(start // BLOCK, (start + count) // BLOCK)
        def _(b):
            row = pl.multiple_of(b * BLOCK, BLOCK)
            azimuth_block(ext, weights, azimuth, m, row, grid_r, grid_t)
            azimuth_block(ext, weights, azimuth, m + 1, row, grid_r, grid_t)

    leftward[0].wait_recv()
    for copy, part in zip(leftward[1:], leftward_rows[1:]):
        copy.wait_recv()
        edge_rows(width - 2, part[0], size)

    for copy in rightward[: len(RELAYS)]:
        copy.wait_recv()
    for copy, part in zip(rightward[len(RELAYS) :], rightward_rows[len(RELAYS) :]):
        copy.wait_recv()
        edge_rows(0, part[0], size)

    for k, mine in enumerate(relays):
        pl.when(mine)(from_relay(k).wait_send)
    pl.when(back_relay)(from_back_relay.wait_send)
    for copy in rightward + leftward:
        copy.wait_send()
    inward.wait_send()
    pl.when(not_outermost)(outward.wait_send)


def write_out(radial_in, azimuth_in, radial, azimuth, sems):
    copies = []
    for k, (src, dst) in enumerate(((radial_in, radial), (azimuth_in, azimuth))):
        copies.append(pltpu.make_async_copy(src, dst, sems.at[k]))
    for copy in copies:
        copy.start()
    for copy in copies:
        copy.wait()


def solution(mesh):
    loop_size, shells = mesh.shape["theta"], mesh.shape["row"]

    def per_device(v):
        _, width, rows, planes = v.shape
        result = jax.ShapeDtypeStruct(v.shape, jnp.bfloat16)
        held = pltpu.VMEM(v.shape, jnp.bfloat16)
        vmem = pl.BlockSpec(memory_space=pltpu.VMEM)
        hbm = pl.BlockSpec(memory_space=pltpu.HBM)
        dma = pltpu.SemaphoreType.DMA
        radial, azimuth = pl.pallas_call(
            functools.partial(tendencies, loop_size, shells),
            out_shape=(held, held),
            in_specs=[hbm],
            out_specs=(vmem, vmem),
            scratch_shapes=[
                pltpu.VMEM((3, width + 4, rows + 2 * PAD, planes), jnp.float32),
                pltpu.VMEM((2, rows, planes), jnp.float32),
                pltpu.VMEM((2, 6 * width, planes), jnp.float32),
                pltpu.VMEM((2, 6 * width, planes), jnp.float32),
                dma,
                dma((2, PIECES + 1)),
                dma((2, PIECES + 1)),
                dma((2,)),
                dma((2,)),
                pltpu.SemaphoreType.REGULAR((4,)),
                pltpu.VMEM((3, 2, max(SHARE, BACK_SHARE), planes), jnp.float32),
                pltpu.SemaphoreType.REGULAR((len(RELAYS) + 1,)),
                pltpu.SemaphoreType.REGULAR,
                dma,
                dma,
            ],
            compiler_params=pltpu.CompilerParams(
                collective_id=0, has_side_effects=True, vmem_limit_bytes=32 << 20
            ),
        )(pltpu.with_memory_space_constraint(v, pltpu.HBM))
        radial = pltpu.with_memory_space_constraint(radial, pltpu.VMEM)
        azimuth = pltpu.with_memory_space_constraint(azimuth, pltpu.VMEM)
        return pl.pallas_call(
            write_out,
            out_shape=(result, result),
            in_specs=[vmem, vmem],
            out_specs=(hbm, hbm),
            scratch_shapes=[dma((2,))],
            compiler_params=pltpu.CompilerParams(vmem_limit_bytes=32 << 20),
        )(radial, azimuth)

    spec = P(None, "theta", "row", None)
    return jax.shard_map(
        per_device, mesh=mesh, in_specs=(spec,), out_specs=(spec, spec), check_vma=False
    )
```
